32 devices in a mesh: tok: 8 (over y, x, core), kv: 4 (over z).
Axes of the slice: x: 2, y: 2, z: 4, core: 2. Of those that a mesh axis runs over, the one named last changes fastest.
Arguments:
- queries: bfloat16 [2048, 8192], P('tok', 'kv'), may hold values from -12 to 12
- key_states: bfloat16 [2048, 1024], P('tok', 'kv'), may hold values from -12 to 12
- value_states: bfloat16 [2048, 1024], P('tok', 'kv'), may hold values from -6 to 6
- doc_lengths: int32 [16], replicated, may hold values from 1 to 1024, 2048 in all
- block_plan: int32 [8, 8], replicated, may hold values from 0 to 7, each once within a row
Outputs:
- attention_out: bfloat16 [2048, 8192], P(('tok', 'kv'))
- served_lse: float32 [64, 2048], P('kv', 'tok')
The draws below stay inside these ranges and needn't reach their ends.
Inputs may be any that keep to these rules, and one draw needn't show every extreme that they name: `doc_lengths`: positive lengths that sum to 2048; the largest is exactly 1024. Every row of block_plan is a permutation of 0 to 7.
All inputs are finite; a program needn't handle non-finite values.
Results may differ from the reference program's by a relative error of at most 0.012.
The reference program's roundings to bfloat16 on the way (of `q_rot`, `k_rot` and `probs`) count: a program that leaves them out, or rounds other values in their place, can miss the bound.
Values may be sent and summed in bfloat16 or wider, within the bound.
No kernel may reach another device: no remote copies, remote signals or barrier semaphores. Data moves between devices by JAX's collectives and lax.ppermute only.
A program may use at most 64 MiB of HBM per device.

```python
import math
import jax
import jax.numpy as jnp
import numpy as np
from jax import lax

HEAD_DIM = 128
Q_HEADS = 64
KV_HEADS = 8
TOK_DEV = 256
DOCS = 16
TOKENS = 2048
LONGEST = 1024
BLOCK = 32
N_TOK = 8


def spread_rows(key, salt, heads):
    row_key = jax.random.fold_in(key, salt)
    scales = jnp.exp(jax.random.uniform(jax.random.fold_in(row_key, 11), (TOKENS, heads, 1), jnp.float32, math.log(0.3), math.log(3.0)))
    noise = jax.random.normal(jax.random.fold_in(row_key, 12), (TOKENS, heads, HEAD_DIM), jnp.float32)
    return jnp.clip(noise * scales, -12.0, 12.0)


def draw_key_states(key, part):
    drawn_draw = spread_rows(key, 301, KV_HEADS)
    return drawn_draw.reshape(TOKENS, KV_HEADS * HEAD_DIM).astype(jnp.bfloat16)


def draw_queries(key, part):
    drawn_draw = spread_rows(key, 302, Q_HEADS)
    return drawn_draw.reshape(TOKENS, Q_HEADS * HEAD_DIM).astype(jnp.bfloat16)


def block_scale(stream_key, extent, split, low, high):
    def one(position, shards_of):
        draws = jax.random.uniform(jax.random.fold_in(jax.random.fold_in(stream_key, 6), position), (shards_of,), jnp.float32, low / len(split), high / len(split))
        return jnp.repeat(jnp.exp(draws), extent[position] // shards_of).reshape((-1,) + (1,) * (len(extent) - position - 1))

    loudness = one(*split[0])
    for cut in split[1:]:
        loudness = loudness * one(*cut)
    return loudness


def profile(count, total, limit, slope):
    portions = [(1 << 20) // math.isqrt(grade ** slope) + 1 for grade in range(2, count + 1)]
    spare, counts = total - limit - (count - 1), [1] * (count - 1)
    while spare > 0:
        candidates = [i for i in range(count - 1) if counts[i] < limit]
        pool, left = sum([portions[i] for i in candidates]), spare
        for i in candidates:
            more = min(limit - counts[i], max(1, left * portions[i] // pool), spare)
            counts[i] = counts[i] + more
            spare = spare - more
    return np.array([limit] + counts)


def ragged_sizes(stream_key, amount, total, reach, skew):
    if amount == 2:
        one = jax.random.randint(stream_key, (), max(1, total - reach), min(reach, total - 1) + 1)
        return jnp.stack([one, total - one])
    lengths = jnp.asarray(profile(amount, total, reach, skew), jnp.int32)
    pairs = (amount - 1) // 2
    giver, sink = lengths[1:1 + 2 * pairs:2], lengths[2:2 + 2 * pairs:2]
    margin = jnp.minimum(giver - 1, reach - sink)
    shifted = jax.random.randint(jax.random.fold_in(stream_key, 1), (pairs,), 0, 1 << 20) % (margin + 1)
    lengths = lengths.at[1:1 + 2 * pairs:2].set(giver - shifted).at[2:2 + 2 * pairs:2].set(sink + shifted)
    return lengths[jax.random.permutation(jax.random.fold_in(stream_key, 2), amount)]


def scatter_about(rng, shape, width, most, pieces=(), kind=jnp.bfloat16):
    drawn = width * jax.random.normal(rng, shape, jnp.float32)
    if pieces:
        drawn = drawn * block_scale(rng, shape, pieces, -0.22, 0.18)
    return jnp.clip(drawn, -most, most).astype(kind)


def setup_inputs(seed: int = 0) -> dict:
    streams_of = jax.random.split(jax.random.key(seed), 6)
    return {
        "queries": draw_queries(jax.random.fold_in(streams_of[5], 71), 0),
        "key_states": draw_key_states(jax.random.fold_in(streams_of[5], 71), 0),
        "value_states": scatter_about(streams_of[2], (TOKENS, KV_HEADS * HEAD_DIM), 1.0, 6.0, ((0, 8), (1, 4))),
        "doc_lengths": ragged_sizes(streams_of[3], DOCS, TOKENS, LONGEST, 2).astype(jnp.int32),
        "block_plan": jax.vmap(lambda own: jax.random.permutation(own, N_TOK))(jax.random.split(streams_of[4], N_TOK)).reshape((N_TOK, N_TOK)).astype(jnp.int32),
    }


THETA = 500000.0

def doc_layout(doc_lengths, token_index):
    doc_ends = jnp.cumsum(doc_lengths).astype(jnp.int32)
    passed = token_index[:, None] >= doc_ends[None, :]
    doc_ids = lax.optimization_barrier(jnp.sum(passed.astype(jnp.int32), axis=1)).astype(jnp.int32)
    starts = lax.optimization_barrier(jnp.sum(jnp.where(passed, doc_lengths[None, :], 0), axis=1)).astype(jnp.int32)
    return (doc_ids, (token_index - starts).astype(jnp.int32))

def rotate(inputs, positions, heads):
    half_dim = HEAD_DIM // 2
    inv_freq = jnp.power(jnp.float32(THETA), -(jnp.arange(half_dim, dtype=jnp.float32) * 2.0 / HEAD_DIM))
    angles = positions.astype(jnp.float32)[:, None] * inv_freq[None, :]
    cosine = jnp.cos(angles)[:, None, :]
    sine_val = jnp.sin(angles)[:, None, :]
    shaped = inputs.astype(jnp.float32).reshape(inputs.shape[0], heads, HEAD_DIM)
    leading = shaped[..., :half_dim]
    trailing = shaped[..., half_dim:]
    turned = jnp.concatenate([leading * cosine - trailing * sine_val, trailing * cosine + leading * sine_val], axis=-1)
    return turned.reshape(inputs.shape[0], heads * HEAD_DIM).astype(jnp.bfloat16)

def reference(queries, key_states, value_states, doc_lengths, block_plan):
    token_index = jnp.arange(TOKENS, dtype=jnp.int32)
    doc_ids, positions = doc_layout(doc_lengths, token_index)
    q_rot = rotate(queries, positions, Q_HEADS)
    k_rot = rotate(key_states, positions, KV_HEADS)
    per_group = Q_HEADS // KV_HEADS
    key_span = (N_TOK // 2 + 1) * TOK_DEV
    score_scale = 1.0 / math.sqrt(HEAD_DIM)

    def one_block(block_id):
        offset = (block_id * TOK_DEV).astype(jnp.int32)
        key_start = jnp.maximum(offset - N_TOK // 2 * TOK_DEV, 0).astype(jnp.int32)
        query_block = lax.dynamic_slice_in_dim(q_rot, offset, TOK_DEV, 0).astype(jnp.float32).reshape(TOK_DEV, KV_HEADS, per_group, HEAD_DIM)
        key_block = lax.dynamic_slice_in_dim(k_rot, key_start, key_span, 0).astype(jnp.float32).reshape(key_span, KV_HEADS, HEAD_DIM)
        value_block = lax.dynamic_slice_in_dim(value_states, key_start, key_span, 0).astype(jnp.float32).reshape(key_span, KV_HEADS, HEAD_DIM)
        scores = jnp.einsum('rgqd,ngd->gqrn', query_block, key_block) * score_scale
        query_index = offset + jnp.arange(TOK_DEV, dtype=jnp.int32)
        key_index = key_start + jnp.arange(key_span, dtype=jnp.int32)
        query_docs = lax.dynamic_slice_in_dim(doc_ids, offset, TOK_DEV, 0)
        key_docs = lax.dynamic_slice_in_dim(doc_ids, key_start, key_span, 0)
        allowed = (query_docs[:, None] == key_docs[None, :]) & (key_index[None, :] <= query_index[:, None])
        scores = jnp.where(allowed, scores, -jnp.inf)
        row_max = lax.optimization_barrier(jnp.max(scores, axis=-1))
        weights = jnp.exp(scores - row_max[..., None])
        row_sum = lax.optimization_barrier(jnp.sum(weights, axis=-1))
        probs = lax.optimization_barrier(weights.astype(jnp.bfloat16)).astype(jnp.float32)
        mixed = jnp.einsum('gqrn,ngd->rgqd', probs, value_block)
        mixed = mixed / jnp.transpose(row_sum, (2, 0, 1))[..., None]
        log_norm = (row_max + jnp.log(row_sum)).reshape(Q_HEADS, TOK_DEV)
        return (mixed.reshape(TOK_DEV, Q_HEADS * HEAD_DIM).astype(jnp.bfloat16), log_norm)
    outputs, norms = lax.map(one_block, jnp.arange(N_TOK, dtype=jnp.int32))
    attention_out = outputs.reshape(TOKENS, Q_HEADS * HEAD_DIM)
    log_all = jnp.transpose(norms, (1, 0, 2)).reshape(Q_HEADS, TOKENS)
    served_order = (jnp.arange(N_TOK, dtype=jnp.int32)[None, :, None] * TOK_DEV + jnp.transpose(block_plan)[:, :, None] * BLOCK + jnp.arange(BLOCK, dtype=jnp.int32)[None, None, :]).reshape(TOKENS).astype(jnp.int32)
    served_lse = jnp.take(log_all, served_order, axis=1)
    return (attention_out, served_lse)
```

```python
import math
from functools import partial

import jax
import jax.numpy as jnp
import numpy as np
from jax import lax
from jax.experimental import pallas as pl
from jax.experimental.pallas import tpu as pltpu
from jax.sharding import PartitionSpec as P

HEAD_DIM = 128
HALF = HEAD_DIM // 2
THETA = 500000.0
NEG = -1e30
LOG2E = math.log2(math.e)
SCALE = 1.0 / math.sqrt(HEAD_DIM)
VMEM_LIMIT = 48 * 1024 * 1024


def vmem():
    return pl.BlockSpec(memory_space=pltpu.VMEM)


def smem():
    return pl.BlockSpec(memory_space=pltpu.SMEM)


def hbm():
    return pl.BlockSpec(memory_space=pl.ANY)


def params():
    return pltpu.CompilerParams(vmem_limit_bytes=VMEM_LIMIT)


def doc_starts(lengths_ref, token):
    begin = jnp.int32(0)
    start = jnp.zeros_like(token)
    for doc in range(lengths_ref.shape[0] - 1):
        begin = begin + lengths_ref[doc]
        start = jnp.where(token >= begin, begin, start)
    return start


def rotary_tables(lengths_ref, freq_ref, rows, first):
    token = first + lax.broadcasted_iota(jnp.int32, (rows, HEAD_DIM), 0)
    position = token - doc_starts(lengths_ref, token)
    angle = position.astype(jnp.float32) * freq_ref[...]
    lane = lax.broadcasted_iota(jnp.int32, (rows, HEAD_DIM), 1)
    sine = jnp.sin(angle)
    return jnp.cos(angle), jnp.where(lane < HALF, -sine, sine)


def turn(block, cosine, sine):
    x = block.astype(jnp.float32)
    return (x * cosine + pltpu.roll(x, HALF, 1) * sine).astype(jnp.bfloat16)


def prepare_kernel(where_ref, lengths_ref, freq_ref, key_ref, value_ref, *out_refs):
    rows = key_ref.shape[0]
    cosine, sine = rotary_tables(lengths_ref, freq_ref, rows, where_ref[0] * rows)
    for group, out_ref in enumerate(out_refs):
        cols = pl.ds(group * HEAD_DIM, HEAD_DIM)
        out_ref[:, 0:HEAD_DIM] = turn(key_ref[:, cols], cosine, sine)
        out_ref[:, HEAD_DIM:] = value_ref[:, cols]


def queries_kernel(where_ref, lengths_ref, freq_ref, query_ref, *out_refs):
    rows = query_ref.shape[0]
    cosine, sine = rotary_tables(lengths_ref, freq_ref, rows, where_ref[0] * rows)
    tiles, stacked, _ = out_refs[0].shape
    tile = rows // tiles
    per_group = stacked // tile
    for group, out_ref in enumerate(out_refs):
        for head in range(per_group):
            cols = pl.ds((group * per_group + head) * HEAD_DIM, HEAD_DIM)
            turned = turn(query_ref[:, cols], cosine, sine)
            for t in range(tiles):
                out_ref[t, head * tile : (head + 1) * tile, :] = turned[t * tile : (t + 1) * tile]


def attend_kernel(pieces, per_group, where_ref, lengths_ref, query_ref, *refs):
    own_ref = refs[0]
    far_refs = refs[1 : 1 + pieces]
    near_refs = refs[1 + pieces : 2 + 2 * pieces]
    refs = refs[2 + 2 * pieces :]
    tiles = query_ref.shape[0]
    out_refs, lse_ref = refs[:tiles], refs[tiles]
    window, scores, sems = refs[tiles + 1 :]
    shard, z = where_ref[0], where_ref[1]
    rows = own_ref.shape[0]
    tile = rows // tiles
    slots = 2 * pieces + 1
    odd = lax.rem(shard, 2) == 1

    def copy(ref, slot):
        return pltpu.make_async_copy(ref, window.at[slot], sems.at[slot])

    fixed = [copy(own_ref, slots - 1)]
    for i in range(1, pieces + 1):
        fixed.append(copy(far_refs[i - 1], slots - 1 - 2 * i))
    for c in fixed:
        c.start()
    for i in range(1, pieces + 1):
        slot = slots - 2 * i

        @pl.when(odd)
        def _():
            copy(near_refs[i - 1], slot).start()

        @pl.when(jnp.logical_not(odd))
        def _():
            copy(near_refs[i], slot).start()

    for c in fixed:
        c.wait()
    for i in range(1, pieces + 1):
        copy(near_refs[i], slots - 2 * i).wait()

    window_first = (shard - (slots - 1)) * rows
    exponent = SCALE * LOG2E
    for s in range(tiles):
        t = lax.rem(z + s, tiles)
        first = shard * rows + t * tile
        token = first + lax.broadcasted_iota(jnp.int32, (tile, rows), 0)
        start = doc_starts(lengths_ref, token)
        lowest = jnp.int32(0)
        begin = jnp.int32(0)
        for doc in range(lengths_ref.shape[0] - 1):
            begin = begin + lengths_ref[doc]
            lowest = jnp.where(first >= begin, begin, lowest)
        low_slot = (lowest - window_first) // rows
        column = lax.broadcasted_iota(jnp.int32, (tile, rows), 1)

        def score_step(slot, highest):
            key = window_first + slot * rows + column
            allowed = (key >= start) & (key <= token)
            keys = window[slot, :, 0:HEAD_DIM]
            result = []
            for head in range(per_group):
                q = query_ref[t, head * tile : (head + 1) * tile, :]
                block = lax.dot_general(
                    q, keys, (((1,), (1,)), ((), ())), preferred_element_type=jnp.float32
                )
                block = jnp.where(allowed, block, NEG)
                scores[slot, head * tile : (head + 1) * tile, :] = block
                best = highest[head]
                for lane in range(0, rows, HEAD_DIM):
                    best = jnp.maximum(best, block[:, lane : lane + HEAD_DIM])
                result.append(best)
            return tuple(result)

        highest = lax.fori_loop(
            low_slot,
            slots,
            score_step,
            tuple(jnp.full((tile, HEAD_DIM), NEG, jnp.float32) for _ in range(per_group)),
        )
        row_max = [jnp.max(h, axis=1, keepdims=True) for h in highest]
        shift = [jnp.broadcast_to(m * exponent, (tile, rows)) for m in row_max]

        def value_step(slot, state):
            sums, totals = state
            values = window[slot, :, HEAD_DIM:]
            new_sums, new_totals = [], []
            for head in range(per_group):
                block = scores[slot, head * tile : (head + 1) * tile, :]
                weights = jnp.exp2(block * exponent - shift[head])
                partial_sum = sums[head]
                for lane in range(0, rows, HEAD_DIM):
                    partial_sum = partial_sum + weights[:, lane : lane + HEAD_DIM]
                new_sums.append(partial_sum)
                new_totals.append(
                    totals[head]
                    + jnp.dot(
                        weights.astype(jnp.bfloat16), values, preferred_element_type=jnp.float32
                    )
                )
            return tuple(new_sums), tuple(new_totals)

        zeros = tuple(jnp.zeros((tile, HEAD_DIM), jnp.float32) for _ in range(per_group))
        sums, totals = lax.fori_loop(low_slot, slots, value_step, (zeros, zeros))
        norms = []
        for head in range(per_group):
            row_sum = jnp.sum(sums[head], axis=1, keepdims=True)
            out_refs[s][:, head * HEAD_DIM : (head + 1) * HEAD_DIM] = (
                totals[head] / row_sum
            ).astype(jnp.bfloat16)
            norms.append(row_max[head] * SCALE + jnp.log(row_sum))
        lse_ref[t] = jnp.concatenate(norms, axis=1)


def assemble_kernel(shards, groups, where_ref, *refs):
    pieces, out_ref, sems = refs[:-2], refs[-2], refs[-1]
    z = where_ref[1]
    width = pieces[0].shape[1]
    copies = []
    for s in range(shards):
        origin = lax.rem(z - s + shards, shards)
        for group in range(groups):
            column = pl.multiple_of((origin * groups + group) * width, width)
            index = s * groups + group
            copies.append(
                pltpu.make_async_copy(
                    pieces[index], out_ref.at[:, pl.ds(column, width)], sems.at[index]
                )
            )
    for c in copies:
        c.start()
    for c in copies:
        c.wait()


def body(queries, key_states, value_states, doc_lengths, block_plan):
    shards = lax.axis_size("tok")
    planes = lax.axis_size("kv")
    shard = lax.axis_index("tok")
    z = lax.axis_index("kv")
    rows = queries.shape[0]
    groups = key_states.shape[1] // HEAD_DIM
    heads = queries.shape[1] // HEAD_DIM
    per_group = heads // groups
    tile = rows // planes
    pieces = shards // 4
    where = jnp.stack([shard, z]).astype(jnp.int32)
    half_freq = THETA ** (-np.arange(HALF, dtype=np.float64) * 2.0 / HEAD_DIM)
    freq = jnp.asarray(np.concatenate([half_freq, half_freq])[None, :], jnp.float32)

    with jax.named_scope("rotate_keys"):
        packed = pl.pallas_call(
            prepare_kernel,
            out_shape=[jax.ShapeDtypeStruct((rows, 2 * HEAD_DIM), jnp.bfloat16)] * groups,
            in_specs=[smem(), smem(), vmem(), vmem(), vmem()],
            out_specs=[vmem()] * groups,
            compiler_params=params(),
        )(where, doc_lengths, freq, key_states, value_states)
    with jax.named_scope("rotate_queries"):
        turned = pl.pallas_call(
            queries_kernel,
            out_shape=[
                jax.ShapeDtypeStruct((planes, per_group * tile, HEAD_DIM), jnp.bfloat16)
            ]
            * groups,
            in_specs=[smem(), smem(), vmem(), vmem()],
            out_specs=[vmem()] * groups,
            compiler_params=params(),
        )(where, doc_lengths, freq, queries)

    pair = [(i, i ^ 1) for i in range(shards)]
    to_odd = [(i, i + 1) for i in range(0, shards, 2)]
    to_even = [(i + 1, i) for i in range(0, shards, 2)]
    outs, norms = [], []
    previous = None
    for group in range(groups):
        own = packed[group]
        if previous is not None:
            own, _ = lax.optimization_barrier((own, previous))
        far = [
            lax.ppermute(own, "tok", [(i, i + 2 * p) for i in range(shards - 2 * p)])
            for p in range(1, pieces + 1)
        ]
        previous = far
        near = [lax.ppermute(own, "tok", to_odd)]
        for p in range(1, pieces):
            near.append(lax.ppermute(far[p - 1], "tok", pair))
        near.append(lax.ppermute(far[pieces - 1], "tok", to_even))
        with jax.named_scope("attend"):
            result = pl.pallas_call(
                partial(attend_kernel, pieces, per_group),
                out_shape=[jax.ShapeDtypeStruct((tile, per_group * HEAD_DIM), jnp.bfloat16)]
                * planes
                + [jax.ShapeDtypeStruct((planes, tile, per_group), jnp.float32)],
                in_specs=[smem(), smem(), vmem()] + [hbm()] * (2 + 2 * pieces),
                out_specs=[vmem()] * (planes + 1),
                scratch_shapes=[
                    pltpu.VMEM((2 * pieces + 1, rows, 2 * HEAD_DIM), jnp.bfloat16),
                    pltpu.VMEM((2 * pieces + 1, per_group * tile, rows), jnp.float32),
                    pltpu.SemaphoreType.DMA((2 * pieces + 1,)),
                ],
                compiler_params=params(),
            )(where, doc_lengths, turned[group], own, *far, *near)
        outs.append(result[:planes])
        norms.append(result[planes])

    received = []
    for group in range(groups):
        row = [outs[group][0]]
        for s in range(1, planes):
            row.append(
                lax.ppermute(
                    outs[group][s], "kv", [(i, (i + s) % planes) for i in range(planes)]
                )
            )
        received.append(row)
    flat = [received[g][s] for s in range(planes) for g in range(groups)]
    with jax.named_scope("assemble"):
        attention_out = pl.pallas_call(
            partial(assemble_kernel, planes, groups),
            out_shape=jax.ShapeDtypeStruct((tile, planes * heads * HEAD_DIM), jnp.bfloat16),
            in_specs=[smem()] + [hbm()] * len(flat),
            out_specs=hbm(),
            scratch_shapes=[pltpu.SemaphoreType.DMA((len(flat),))],
            compiler_params=params(),
        )(where, *flat)

    block_rows = rows // shards
    log_norm = jnp.concatenate([n.reshape(rows, per_group) for n in norms], axis=1)
    my_blocks = lax.dynamic_index_in_dim(block_plan, shard, 0, keepdims=False)
    outgoing = jnp.take(log_norm.reshape(shards, block_rows, heads), my_blocks, axis=0)
    served = lax.all_to_all(outgoing, "tok", split_axis=0, concat_axis=0, tiled=True)
    served_lse = served.reshape(rows, heads).T
    return (attention_out, served_lse)


def solution(mesh):
    return jax.shard_map(
        body,
        mesh=mesh,
        in_specs=(P("tok", "kv"), P("tok", "kv"), P("tok", "kv"), P(), P()),
        out_specs=(P(("tok", "kv"), None), P("kv", "tok")),
        check_vma=False,
    )
```

```python
import math
from functools import partial

import jax
import jax.numpy as jnp
import numpy as np
from jax import lax
from jax.experimental import pallas as pl
from jax.experimental.pallas import tpu as pltpu
from jax.sharding import PartitionSpec as P

HEAD_DIM = 128
HALF = HEAD_DIM // 2
THETA = 500000.0
NEG = -1e30
LOG2E = math.log2(math.e)
SCALE = 1.0 / math.sqrt(HEAD_DIM)
VMEM_LIMIT = 48 * 1024 * 1024


def vmem():
    return pl.BlockSpec(memory_space=pltpu.VMEM)


def smem():
    return pl.BlockSpec(memory_space=pltpu.SMEM)


def hbm():
    return pl.BlockSpec(memory_space=pl.ANY)


def far_hbm():
    return pl.BlockSpec(memory_space=pltpu.HBM)


def params():
    return pltpu.CompilerParams(vmem_limit_bytes=VMEM_LIMIT)


def cost(microseconds):
    return pl.CostEstimate(flops=int(microseconds * 1.15e9), bytes_accessed=0, transcendentals=0)


def doc_starts(lengths_ref, token):
    begin = jnp.int32(0)
    start = jnp.zeros_like(token)
    for doc in range(lengths_ref.shape[0] - 1):
        begin = begin + lengths_ref[doc]
        start = jnp.where(token >= begin, begin, start)
    return start


def rotary_tables(lengths_ref, freq_ref, rows, first):
    token = first + lax.broadcasted_iota(jnp.int32, (rows, HEAD_DIM), 0)
    start = doc_starts(lengths_ref, token)
    position = token - start
    angle = position.astype(jnp.float32) * freq_ref[...]
    lane = lax.broadcasted_iota(jnp.int32, (rows, HEAD_DIM), 1)
    sine = jnp.sin(angle)
    return jnp.cos(angle), jnp.where(lane < HALF, -sine, sine), start


def turn(block, cosine, sine):
    x = block.astype(jnp.float32)
    return (x * cosine + pltpu.roll(x, HALF, 1) * sine).astype(jnp.bfloat16)


def pack_keys(out_ref, key_ref, value_ref, cosine, sine):
    out_ref[:, 0:HEAD_DIM] = turn(key_ref[...], cosine, sine)
    out_ref[:, HEAD_DIM:] = value_ref[...]


def group_copies(key_hbm, value_hbm, key_ref, value_ref, sems, group):
    cols = pl.ds(group * HEAD_DIM, HEAD_DIM)
    return [
        pltpu.make_async_copy(key_hbm.at[:, cols], key_ref, sems.at[0]),
        pltpu.make_async_copy(value_hbm.at[:, cols], value_ref, sems.at[1]),
    ]


def keys_kernel(where_ref, lengths_hbm, freq_hbm, key_hbm, value_hbm, out_ref, *scratch):
    lengths_ref, freq_ref, key_ref, value_ref, sems, table_sems = scratch
    tables = [
        pltpu.make_async_copy(lengths_hbm, lengths_ref, table_sems.at[0]),
        pltpu.make_async_copy(freq_hbm, freq_ref, table_sems.at[1]),
    ]
    copies = group_copies(key_hbm, value_hbm, key_ref, value_ref, sems, 0)
    for c in tables + copies:
        c.start()
    for c in tables:
        c.wait()
    rows = key_ref.shape[0]
    cosine, sine, _ = rotary_tables(lengths_ref, freq_ref, rows, where_ref[0] * rows)
    for c in copies:
        c.wait()
    pack_keys(out_ref, key_ref, value_ref, cosine, sine)


def queries_kernel(where_ref, lengths_ref, freq_ref, key_hbm, value_hbm, query_hbm, after, *refs):
    groups = (len(refs) - 5) // 2
    pack_refs, turn_refs = refs[: groups - 1], refs[groups - 1 : 2 * groups - 1]
    start_ref, key_ref, value_ref, query_ref, sems, query_sem = refs[2 * groups - 1 :]
    query_copy = pltpu.make_async_copy(query_hbm, query_ref, query_sem.at[0])
    query_copy.start()
    rows = query_ref.shape[0]
    for group in range(1, groups):
        for c in group_copies(
            key_hbm, value_hbm, key_ref.at[group - 1], value_ref.at[group - 1],
            sems.at[group - 1], group,
        ):
            c.start()
    cosine, sine, start = rotary_tables(lengths_ref, freq_ref, rows, where_ref[0] * rows)
    start_ref[...] = start
    for group in range(1, groups):
        for c in group_copies(
            key_hbm, value_hbm, key_ref.at[group - 1], value_ref.at[group - 1],
            sems.at[group - 1], group,
        ):
            c.wait()
        pack_keys(
            pack_refs[group - 1], key_ref.at[group - 1], value_ref.at[group - 1], cosine, sine
        )
    query_copy.wait()
    tiles, stacked, _ = turn_refs[0].shape
    tile = rows // tiles
    per_group = stacked // tile
    for group, out_ref in enumerate(turn_refs):
        for head in range(per_group):
            cols = pl.ds((group * per_group + head) * HEAD_DIM, HEAD_DIM)
            turned = turn(query_ref[:, cols], cosine, sine)
            for t in range(tiles):
                out_ref[t, head * tile : (head + 1) * tile, :] = turned[t * tile : (t + 1) * tile]


def key_counts(slots):
    return sorted({-(-slots * k // 5) for k in range(1, 6)})


def attend_kernel(pieces, per_group, groups, tiles_of, begun, last, where_ref, *refs):
    lengths_ref, plan_ref, start_ref = refs[:3]
    refs = refs[3:]
    norm_ref = None
    if begun:
        norm_ref, refs = refs[0], refs[1:]
    slots = 2 * pieces + 1
    tasks = len(groups) * len(tiles_of)
    query_refs, own_refs, far_refs, near_refs = {}, {}, {}, {}
    for group in groups:
        query_refs[group], own_refs[group] = refs[:2]
        far_refs[group] = refs[2 : 2 + pieces]
        near_refs[group] = refs[2 + pieces : 3 + 2 * pieces]
        refs = refs[3 + 2 * pieces :]
    out_refs, lse_ref = refs[:tasks], refs[tasks]
    staged, chosen, norms = refs[tasks + 1 :]
    shard, z = where_ref[0], where_ref[1]
    tiles, stacked, _ = query_refs[groups[0]].shape
    tile = stacked // per_group
    rows = tile * tiles
    odd = lax.rem(shard, 2) == 1
    for position, group in enumerate(groups):
        for i in range(1, pieces + 1):

            @pl.when(odd)
            def _():
                chosen[position, i - 1] = near_refs[group][i - 1][...]

            @pl.when(jnp.logical_not(odd))
            def _():
                chosen[position, i - 1] = near_refs[group][i][...]

    def window(group, slot, cols):
        back = slots - 1 - slot
        if back == 0:
            return own_refs[group][:, cols]
        if back % 2 == 0:
            return far_refs[group][back // 2 - 1][:, cols]
        return chosen[groups.index(group), (back + 1) // 2 - 1, :, cols]

    first = shard * rows
    lowest = jnp.int32(0)
    begin = jnp.int32(0)
    for doc in range(lengths_ref.shape[0] - 1):
        begin = begin + lengths_ref[doc]
        lowest = jnp.where(first >= begin, begin, lowest)
    window_first = (shard - (slots - 1)) * rows
    count = slots - (lowest - window_first) // rows
    exponent = SCALE * LOG2E
    column = lax.broadcasted_iota(jnp.int32, (tile, HEAD_DIM), 1)
    line = lax.broadcasted_iota(jnp.int32, (tile, HEAD_DIM), 0)
    chunk = min(stacked, 256)
    inside = chunk // tile
    key_cols = slice(0, HEAD_DIM)
    value_cols = slice(HEAD_DIM, 2 * HEAD_DIM)
    norms[...] = norm_ref[...] if begun else jnp.zeros(norms.shape, jnp.float32)

    def one(n, group, s, position):
        t = lax.rem(z + s, tiles)
        here = pl.ds(pl.multiple_of(t * tile, tile), tile)
        start = start_ref[here, :]
        gathered = norms[here, :]
        for c in range(stacked // chunk):
            q = query_refs[group][t, c * chunk : (c + 1) * chunk, :]
            parts, best = [], None
            for slot in range(slots - n, slots):
                block = lax.dot_general(
                    q,
                    window(group, slot, key_cols),
                    (((1,), (1,)), ((), ())),
                    preferred_element_type=jnp.float32,
                )
                begins = start - (window_first + slot * rows)
                for lane in range(0, rows, HEAD_DIM):
                    allowed = column + lane >= begins
                    if slot == slots - 1:
                        allowed = allowed & (column + lane <= line + t * tile)
                    part = block[:, lane : lane + HEAD_DIM].reshape(inside, tile, HEAD_DIM)
                    part = jnp.where(allowed[None], part, NEG).reshape(chunk, HEAD_DIM)
                    parts.append(part)
                    best = part if best is None else jnp.maximum(best, part)
            top = jnp.max(best, axis=1, keepdims=True) * exponent
            total, mixed = None, None
            per_slot = rows // HEAD_DIM
            for i, slot in enumerate(range(slots - n, slots)):
                probs = []
                for part in parts[per_slot * i : per_slot * (i + 1)]:
                    weights = jnp.exp2(part * exponent - top)
                    total = weights if total is None else total + weights
                    probs.append(weights.astype(jnp.bfloat16))
                product = jnp.dot(
                    jnp.concatenate(probs, axis=1),
                    window(group, slot, value_cols),
                    preferred_element_type=jnp.float32,
                )
                mixed = product if mixed is None else mixed + product
            row_sum = jnp.sum(total, axis=1, keepdims=True)
            result = (mixed / row_sum).astype(jnp.bfloat16)
            norm = top * (1.0 / LOG2E) + jnp.log(row_sum)
            for h in range(inside):
                head = c * inside + h
                part = slice(h * tile, (h + 1) * tile)
                staged[position, :, head * HEAD_DIM : (head + 1) * HEAD_DIM] = result[part]
                gathered = jnp.where(column == group * per_group + head, norm[part], gathered)
        norms[here, :] = gathered

    counts = key_counts(slots)
    for low, n in zip([0] + counts, counts):

        @pl.when((count > low) & (count <= n))
        def _():
            for position, group in enumerate(groups):

                def step(i, carry):
                    s = tiles_of.start + i * tiles_of.step
                    one(n, group, s, position * len(tiles_of) + i)
                    return carry

                lax.fori_loop(0, len(tiles_of), step, 0, unroll=n <= 5)

    for position, out_ref in enumerate(out_refs):
        out_ref[...] = staged[position]
    if last:
        shards = plan_ref.shape[0]
        block = rows // shards
        for s in range(shards):
            picked = pl.multiple_of(plan_ref[shard, s] * block, block)
            lse_ref[s * block : (s + 1) * block, :] = norms[pl.ds(picked, block), :]
    else:
        lse_ref[...] = norms[...]


def assemble_kernel(shards, groups, where_ref, served_ref, *refs):
    pieces, out_ref, lse_ref, sems = refs[:-3], refs[-3], refs[-2], refs[-1]
    z = where_ref[1]
    width = pieces[0].shape[1]
    copies = []
    for s in range(shards):
        origin = lax.rem(z - s + shards, shards)
        for group in range(groups):
            column = pl.multiple_of((origin * groups + group) * width, width)
            index = s * groups + group
            copies.append(
                pltpu.make_async_copy(
                    pieces[index], out_ref.at[:, pl.ds(column, width)], sems.at[index]
                )
            )
    for c in copies:
        c.start()
    lse_ref[...] = served_ref[...].T[: lse_ref.shape[0]]
    for c in copies:
        c.wait()


def body(queries, key_states, value_states, doc_lengths, block_plan):
    shards = lax.axis_size("tok")
    planes = lax.axis_size("kv")
    shard = lax.axis_index("tok")
    z = lax.axis_index("kv")
    rows = queries.shape[0]
    groups = key_states.shape[1] // HEAD_DIM
    heads = queries.shape[1] // HEAD_DIM
    per_group = heads // groups
    tile = rows // planes
    pieces = shards // 4
    where = jnp.stack([shard, z]).astype(jnp.int32)
    half_freq = THETA ** (-np.arange(HALF, dtype=np.float64) * 2.0 / HEAD_DIM)
    freq = jnp.asarray(np.concatenate([half_freq, half_freq])[None, :], jnp.float32)

    fixed_keys = pltpu.with_memory_space_constraint(key_states, pltpu.HBM)
    fixed_values = pltpu.with_memory_space_constraint(value_states, pltpu.HBM)
    fixed_queries = pltpu.with_memory_space_constraint(queries, pltpu.HBM)
    pack_shape = jax.ShapeDtypeStruct((rows, 2 * HEAD_DIM), jnp.bfloat16)
    half = pltpu.VMEM((rows, HEAD_DIM), jnp.bfloat16)
    with jax.named_scope("rotate_keys"):
        first_pack = pl.pallas_call(
            keys_kernel,
            out_shape=pack_shape,
            in_specs=[smem(), hbm(), hbm(), hbm(), hbm()],
            out_specs=vmem(),
            scratch_shapes=[
                pltpu.SMEM(doc_lengths.shape, jnp.int32),
                pltpu.VMEM(freq.shape, jnp.float32),
                half,
                half,
                pltpu.SemaphoreType.DMA((2,)),
                pltpu.SemaphoreType.DMA((2,)),
            ],
            compiler_params=params(),
            cost_estimate=cost(1.0),
        )(
            where,
            pltpu.with_memory_space_constraint(doc_lengths, pltpu.HBM),
            pltpu.with_memory_space_constraint(freq, pltpu.HBM),
            fixed_keys,
            fixed_values,
        )
    halves = pltpu.VMEM((groups - 1, rows, HEAD_DIM), jnp.bfloat16)
    with jax.named_scope("rotate_queries"):
        result = pl.pallas_call(
            queries_kernel,
            out_shape=[pack_shape] * (groups - 1)
            + [jax.ShapeDtypeStruct((planes, per_group * tile, HEAD_DIM), jnp.bfloat16)] * groups
            + [jax.ShapeDtypeStruct((rows, HEAD_DIM), jnp.int32)],
            in_specs=[smem(), smem(), vmem(), hbm(), hbm(), hbm(), hbm()],
            out_specs=[vmem()] * (2 * groups),
            scratch_shapes=[
                halves,
                halves,
                pltpu.VMEM(queries.shape, jnp.bfloat16),
                pltpu.SemaphoreType.DMA((groups - 1, 2)),
                pltpu.SemaphoreType.DMA((1,)),
            ],
            compiler_params=params(),
            cost_estimate=cost(2.0),
        )(where, doc_lengths, freq, fixed_keys, fixed_values, fixed_queries, first_pack)
    packed = [first_pack, *result[: groups - 1]]
    turned = result[groups - 1 : 2 * groups - 1]
    start = result[2 * groups - 1]

    pair = [(i, i ^ 1) for i in range(shards)]
    to_odd = [(i, i + 1) for i in range(0, shards, 2)]
    to_even = [(i + 1, i) for i in range(0, shards, 2)]
    far, near = [], []

    def attend(norm, used, tiles_of, last, microseconds):
        operands = [start] if norm is None else [start, norm]
        for group in used:
            operands += [turned[group], packed[group], *far[group], *near[group]]
        tasks = len(used) * len(tiles_of)
        with jax.named_scope("attend"):
            result = pl.pallas_call(
                partial(
                    attend_kernel, pieces, per_group, used, tiles_of, norm is not None, last
                ),
                out_shape=[jax.ShapeDtypeStruct((tile, per_group * HEAD_DIM), jnp.bfloat16)]
                * tasks
                + [jax.ShapeDtypeStruct((rows, HEAD_DIM), jnp.float32)],
                in_specs=[smem(), smem(), smem()] + [vmem()] * len(operands),
                out_specs=[vmem()] * (tasks + 1),
                scratch_shapes=[
                    pltpu.VMEM((tasks, tile, per_group * HEAD_DIM), jnp.bfloat16),
                    pltpu.VMEM((len(used), pieces, rows, 2 * HEAD_DIM), jnp.bfloat16),
                    pltpu.VMEM((rows, HEAD_DIM), jnp.float32),
                ],
                compiler_params=params(),
                cost_estimate=cost(microseconds),
            )(where, doc_lengths, block_plan, *operands)
        return result[:tasks], result[tasks]

    def send(piece, s):
        return lax.ppermute(piece, "kv", [(i, (i + s) % planes) for i in range(planes)])

    for group in range(groups):
        own = packed[group]
        far.append(
            [
                lax.ppermute(own, "tok", [(i, i + 2 * p) for i in range(shards - 2 * p)])
                for p in range(1, pieces + 1)
            ]
        )
    middle = planes // 2
    norm = None
    received = [[None] * planes for _ in range(groups)]
    for group in range(groups):
        mine, theirs = packed[group], far[group]
        if group:
            theirs, _ = lax.optimization_barrier((theirs, norm))
        mine, _ = lax.optimization_barrier((mine, start))
        near.append([lax.ppermute(mine, "tok", to_odd)])
        for p in range(1, pieces):
            near[group].append(lax.ppermute(theirs[p - 1], "tok", pair))
        near[group].append(lax.ppermute(theirs[pieces - 1], "tok", to_even))
        if group == 0:
            spans = [range(middle, middle + 1), range(1, planes, 2)]
            spans += [range(s, s + 1) for s in range(2, planes, 2) if s != middle]
        else:
            spans = [range(1, planes)]
            norm, _ = lax.optimization_barrier((norm, received[group - 1][middle]))
        for span in spans:
            result, norm = attend(norm, [group], span, False, 2.0 * len(span))
            for s, piece in zip(span, result):
                received[group][s] = send(piece, s)
    result, norm = attend(norm, list(range(groups)), range(1), True, 3.0)
    for group in range(groups):
        received[group][0] = result[group]
    block_rows = rows // shards
    served = lax.all_to_all(
        norm.reshape(shards, block_rows, HEAD_DIM), "tok", split_axis=0, concat_axis=0, tiled=True
    ).reshape(rows, HEAD_DIM)
    flat = [received[g][s] for s in range(planes) for g in range(groups)]
    with jax.named_scope("assemble"):
        attention_out, served_lse = pl.pallas_call(
            partial(assemble_kernel, planes, groups),
            out_shape=[
                jax.ShapeDtypeStruct((tile, planes * heads * HEAD_DIM), jnp.bfloat16),
                jax.ShapeDtypeStruct((heads, rows), jnp.float32),
            ],
            in_specs=[smem(), vmem()] + [hbm()] * len(flat),
            out_specs=[hbm(), vmem()],
            scratch_shapes=[pltpu.SemaphoreType.DMA((len(flat),))],
            compiler_params=params(),
        )(where, served, *flat)
    return (attention_out, served_lse)


def solution(mesh):
    return jax.shard_map(
        body,
        mesh=mesh,
        in_specs=(P("tok", "kv"), P("tok", "kv"), P("tok", "kv"), P(), P()),
        out_specs=(P(("tok", "kv"), None), P("kv", "tok")),
        check_vma=False,
    )
```

```python
import math
from functools import partial

import jax
import jax.numpy as jnp
import numpy as np
from jax import lax
from jax.experimental import pallas as pl
from jax.experimental.pallas import tpu as pltpu
from jax.sharding import PartitionSpec as P

HEAD_DIM = 128
HALF = HEAD_DIM // 2
THETA = 500000.0
NEG = -1e30
LOG2E = math.log2(math.e)
SCALE = 1.0 / math.sqrt(HEAD_DIM)
VMEM_LIMIT = 48 * 1024 * 1024


def vmem():
    return pl.BlockSpec(memory_space=pltpu.VMEM)


def smem():
    return pl.BlockSpec(memory_space=pltpu.SMEM)


def hbm():
    return pl.BlockSpec(memory_space=pl.ANY)


def far_hbm():
    return pl.BlockSpec(memory_space=pltpu.HBM)


def params():
    return pltpu.CompilerParams(vmem_limit_bytes=VMEM_LIMIT)


def cost(microseconds):
    return pl.CostEstimate(flops=int(microseconds * 1.15e9), bytes_accessed=0, transcendentals=0)


def doc_starts(lengths_ref, token):
    begin = jnp.int32(0)
    start = jnp.zeros_like(token)
    for doc in range(lengths_ref.shape[0] - 1):
        begin = begin + lengths_ref[doc]
        start = jnp.where(token >= begin, begin, start)
    return start


def rotary_tables(lengths_ref, freq_ref, rows, first):
    token = first + lax.broadcasted_iota(jnp.int32, (rows, HEAD_DIM), 0)
    start = doc_starts(lengths_ref, token)
    position = token - start
    angle = position.astype(jnp.float32) * freq_ref[...]
    lane = lax.broadcasted_iota(jnp.int32, (rows, HEAD_DIM), 1)
    sine = jnp.sin(angle)
    return jnp.cos(angle), jnp.where(lane < HALF, -sine, sine), start


def turn(block, cosine, sine):
    x = block.astype(jnp.float32)
    return (x * cosine + pltpu.roll(x, HALF, 1) * sine).astype(jnp.bfloat16)


def pack(out_ref, key_ref, value_ref, cosine, sine):
    for group in range(key_ref.shape[1] // HEAD_DIM):
        cols = slice(group * HEAD_DIM, (group + 1) * HEAD_DIM)
        place = 2 * group * HEAD_DIM
        out_ref[:, place : place + HEAD_DIM] = turn(key_ref[:, cols], cosine, sine)
        out_ref[:, place + HEAD_DIM : place + 2 * HEAD_DIM] = value_ref[:, cols]


def queries_kernel(pieces, where_ref, lengths_ref, freq_ref, key_hbm, value_hbm, query_hbm, *refs):
    pack_ref, start_ref, table_ref = refs[:3]
    turn_refs = refs[3:-4]
    key_ref, value_ref, query_ref, sems = refs[-4:]
    copies = [
        pltpu.make_async_copy(key_hbm, key_ref, sems.at[0]),
        pltpu.make_async_copy(value_hbm, value_ref, sems.at[1]),
        pltpu.make_async_copy(query_hbm, query_ref, sems.at[2]),
    ]
    for c in copies:
        c.start()
    rows = query_ref.shape[0]
    shard = where_ref[0]
    cosine, sine, start = rotary_tables(lengths_ref, freq_ref, rows, shard * rows)
    start_ref[...] = start
    for c in copies[:2]:
        c.wait()
    pack(pack_ref, key_ref, value_ref, cosine, sine)
    copies[2].wait()
    tiles, stacked, _ = turn_refs[0].shape
    tile = rows // tiles
    per_group = stacked // tile
    for group, out_ref in enumerate(turn_refs):
        for head in range(per_group):
            cols = pl.ds((group * per_group + head) * HEAD_DIM, HEAD_DIM)
            turned = turn(query_ref[:, cols], cosine, sine)
            for t in range(tiles):
                out_ref[t, head * tile : (head + 1) * tile, :] = turned[t * tile : (t + 1) * tile]
    for p in range(1, pieces + 1):
        cosine, sine, _ = rotary_tables(lengths_ref, freq_ref, rows, (shard - 2 * p) * rows)
        table_ref[2 * p - 2] = cosine
        table_ref[2 * p - 1] = sine


def pack_kernel(table_ref, *refs):
    pieces = len(refs) // 2
    for p in range(pieces):
        pack(
            refs[2 * pieces].at[p],
            refs[p],
            refs[pieces + p],
            table_ref[2 * p],
            table_ref[2 * p + 1],
        )


def attend_kernel(pieces, per_group, groups, tiles_of, begun, last, where_ref, *refs):
    plan_ref = norm_ref = None
    if last:
        plan_ref, refs = refs[0], refs[1:]
    start_ref, refs = refs[0], refs[1:]
    if begun:
        norm_ref, refs = refs[0], refs[1:]
    slots = 2 * pieces + 1
    tasks = len(tiles_of)
    own_ref, beside_ref, far_ref, near_ref = refs[:4]
    refs = refs[4:]
    query_refs, refs = dict(zip(groups, refs)), refs[len(groups) :]
    out_refs, lse_ref = refs[:tasks], refs[tasks]
    staged, chosen, norms = refs[tasks + 1 :]
    shard, z = where_ref[0], where_ref[1]
    tiles, stacked, _ = query_refs[groups[0]].shape
    tile = stacked // per_group
    rows = tile * tiles
    odd = lax.rem(shard, 2) == 1
    used = slice(2 * groups[0] * HEAD_DIM, 2 * (groups[-1] + 1) * HEAD_DIM)
    for i in range(1, pieces + 1):

        @pl.when(odd)
        def _():
            before = beside_ref if i == 1 else near_ref.at[i - 2]
            chosen[i - 1, :, used] = before[:, used]

        @pl.when(jnp.logical_not(odd))
        def _():
            chosen[i - 1, :, used] = near_ref[i - 1, :, used]

    def window(group, slot, part):
        place = (2 * group + part) * HEAD_DIM
        cols = slice(place, place + HEAD_DIM)
        back = slots - 1 - slot
        if back == 0:
            return own_ref[:, cols]
        if back % 2 == 0:
            return far_ref[back // 2 - 1, :, cols]
        return chosen[(back + 1) // 2 - 1, :, cols]

    first = shard * rows
    window_first = (shard - (slots - 1)) * rows
    exponent = SCALE * LOG2E
    column = lax.broadcasted_iota(jnp.int32, (tile, HEAD_DIM), 1)
    line = lax.broadcasted_iota(jnp.int32, (tile, HEAD_DIM), 0)
    chunk = min(stacked, 256)
    inside = chunk // tile
    norms[...] = norm_ref[...] if begun else jnp.zeros(norms.shape, jnp.float32)

    def masks_of(t):
        start = start_ref[pl.ds(pl.multiple_of(t * tile, tile), tile), :]
        masks = []
        for slot in range(slots):
            begins = start - (window_first + slot * rows)
            for lane in range(0, rows, HEAD_DIM):
                allowed = column + lane >= begins
                if slot == slots - 1:
                    allowed = allowed & (column + lane <= line + t * tile)
                masks.append(allowed[None])
        return masks

    def scores_of(group, t, c, masks):
        q = query_refs[group][t, c * chunk : (c + 1) * chunk, :]
        parts, best = [], None
        for slot in range(slots):
            block = lax.dot_general(
                q,
                window(group, slot, 0),
                (((1,), (1,)), ((), ())),
                preferred_element_type=jnp.float32,
            )
            for lane in range(0, rows, HEAD_DIM):
                part = block[:, lane : lane + HEAD_DIM].reshape(inside, tile, HEAD_DIM)
                part = jnp.where(masks[len(parts)], part, NEG).reshape(chunk, HEAD_DIM)
                parts.append(part)
                best = part if best is None else jnp.maximum(best, part)
        return parts, best

    def mix(index, c, i, parts, best, gathered):
        group = groups[index]
        top = jnp.max(best, axis=1, keepdims=True) * exponent
        total, mixed = None, None
        per_slot = rows // HEAD_DIM
        for slot in range(slots):
            probs = []
            for part in parts[per_slot * slot : per_slot * (slot + 1)]:
                weights = jnp.exp2(part * exponent - top)
                total = weights if total is None else total + weights
                probs.append(weights.astype(jnp.bfloat16))
            product = jnp.dot(
                jnp.concatenate(probs, axis=1),
                window(group, slot, 1),
                preferred_element_type=jnp.float32,
            )
            mixed = product if mixed is None else mixed + product
        row_sum = jnp.sum(total, axis=1, keepdims=True)
        result = (mixed / row_sum).astype(jnp.bfloat16)
        norm = top * (1.0 / LOG2E) + jnp.log(row_sum)
        for h in range(inside):
            head = c * inside + h
            part = slice(h * tile, (h + 1) * tile)
            column_of = (index * per_group + head) * HEAD_DIM
            staged[i, :, column_of : column_of + HEAD_DIM] = result[part]
            gathered = jnp.where(column == group * per_group + head, norm[part], gathered)
        return gathered

    def step(i, carry):
        t = lax.rem(z + tiles_of.start + i * tiles_of.step, tiles)
        here = pl.ds(pl.multiple_of(t * tile, tile), tile)
        gathered = norms[here, :]
        masks = masks_of(t)
        jobs = [(index, c) for index in range(len(groups)) for c in range(stacked // chunk)]
        ready = scores_of(groups[0], t, 0, masks)
        for job, (index, c) in enumerate(jobs):
            following = None
            if job + 1 < len(jobs):
                next_index, next_c = jobs[job + 1]
                following = scores_of(groups[next_index], t, next_c, masks)
            gathered = mix(index, c, i, *ready, gathered)
            ready = following
        norms[here, :] = gathered
        return carry

    lax.fori_loop(0, len(tiles_of), step, 0, unroll=slots <= 5)

    for position, out_ref in enumerate(out_refs):
        out_ref[...] = staged[position]
    if last:
        shards = plan_ref.shape[0]
        block = rows // shards
        for s in range(shards):
            picked = pl.multiple_of(plan_ref[shard, s] * block, block)
            lse_ref[s * block : (s + 1) * block, :] = norms[pl.ds(picked, block), :]
    else:
        lse_ref[...] = norms[...]


def assemble_kernel(planes, width, groups, places, where_ref, served_ref, *refs):
    pieces, out_ref, lse_hbm, lse_ref, sems = refs[:-4], *refs[-4:]
    z = where_ref[1]
    copies = []
    for index, (s, group) in enumerate(places):
        origin = lax.rem(z - s + planes, planes)
        column = pl.multiple_of((origin * groups + group) * width, width)
        target = out_ref.at[:, pl.ds(column, pieces[index].shape[1])]
        copies.append(pltpu.make_async_copy(pieces[index], target, sems.at[index]))
    for c in copies:
        c.start()
    lse_ref[...] = served_ref[...].T[: lse_ref.shape[0]]
    lse_copy = pltpu.make_async_copy(lse_ref, lse_hbm, sems.at[len(pieces)])
    lse_copy.start()
    for c in copies:
        c.wait()
    lse_copy.wait()


def body(queries, key_states, value_states, doc_lengths, block_plan):
    shards = lax.axis_size("tok")
    planes = lax.axis_size("kv")
    shard = lax.axis_index("tok")
    z = lax.axis_index("kv")
    rows = queries.shape[0]
    groups = key_states.shape[1] // HEAD_DIM
    heads = queries.shape[1] // HEAD_DIM
    per_group = heads // groups
    tile = rows // planes
    pieces = shards // 4
    where = jnp.stack([shard, z]).astype(jnp.int32)
    half_freq = THETA ** (-np.arange(HALF, dtype=np.float64) * 2.0 / HEAD_DIM)
    freq = jnp.asarray(np.concatenate([half_freq, half_freq])[None, :], jnp.float32)

    pair = [(i, i ^ 1) for i in range(shards)]
    to_odd = [(i, i + 1) for i in range(0, shards, 2)]
    arrived = [
        [
            lax.ppermute(x, "tok", [(i, i + 2 * p) for i in range(shards - 2 * p)])
            for p in range(1, pieces + 1)
        ]
        for x in (key_states, value_states)
    ]
    pack_shape = jax.ShapeDtypeStruct((rows, 2 * groups * HEAD_DIM), jnp.bfloat16)
    with jax.named_scope("rotate"):
        result = pl.pallas_call(
            partial(queries_kernel, pieces),
            out_shape=[
                pack_shape,
                jax.ShapeDtypeStruct((rows, HEAD_DIM), jnp.int32),
                jax.ShapeDtypeStruct((2 * pieces, rows, HEAD_DIM), jnp.float32),
            ]
            + [jax.ShapeDtypeStruct((planes, per_group * tile, HEAD_DIM), jnp.bfloat16)] * groups,
            in_specs=[smem(), smem(), vmem(), hbm(), hbm(), hbm()],
            out_specs=[vmem()] * (3 + groups),
            scratch_shapes=[
                pltpu.VMEM(key_states.shape, jnp.bfloat16),
                pltpu.VMEM(value_states.shape, jnp.bfloat16),
                pltpu.VMEM(queries.shape, jnp.bfloat16),
                pltpu.SemaphoreType.DMA((3,)),
            ],
            compiler_params=params(),
            cost_estimate=cost(3.0),
        )(
            where,
            doc_lengths,
            freq,
            pltpu.with_memory_space_constraint(key_states, pltpu.HBM),
            pltpu.with_memory_space_constraint(value_states, pltpu.HBM),
            pltpu.with_memory_space_constraint(queries, pltpu.HBM),
        )
    own, start, tables = result[:3]
    turned = result[3:]
    beside = lax.ppermute(own, "tok", to_odd)
    tables, beside = lax.optimization_barrier((tables, beside))
    with jax.named_scope("pack"):
        far = pl.pallas_call(
            pack_kernel,
            out_shape=jax.ShapeDtypeStruct((pieces, *pack_shape.shape), jnp.bfloat16),
            in_specs=[vmem()] * (1 + 2 * pieces),
            out_specs=vmem(),
            compiler_params=params(),
            cost_estimate=cost(1.0),
        )(tables, *arrived[0], *arrived[1])
    near = lax.ppermute(far, "tok", pair)

    def attend(norm, used, tiles_of, last, microseconds):
        scalars = [where, block_plan] if last else [where]
        operands = [start] if norm is None else [start, norm]
        operands += [own, beside, far, near] + [turned[group] for group in used]
        tasks = len(tiles_of)
        width = len(used) * per_group * HEAD_DIM
        with jax.named_scope("attend"):
            result = pl.pallas_call(
                partial(
                    attend_kernel, pieces, per_group, used, tiles_of, norm is not None, last
                ),
                out_shape=[jax.ShapeDtypeStruct((tile, width), jnp.bfloat16)]
                * tasks
                + [jax.ShapeDtypeStruct((rows, HEAD_DIM), jnp.float32)],
                in_specs=[smem()] * len(scalars) + [vmem()] * len(operands),
                out_specs=[vmem()] * (tasks + 1),
                scratch_shapes=[
                    pltpu.VMEM((tasks, tile, width), jnp.bfloat16),
                    pltpu.VMEM((pieces, *pack_shape.shape), jnp.bfloat16),
                    pltpu.VMEM((rows, HEAD_DIM), jnp.float32),
                ],
                compiler_params=params(),
                cost_estimate=cost(microseconds),
            )(*scalars, *operands)
        return result[:tasks], result[tasks]

    def send(piece, s):
        return lax.ppermute(piece, "kv", [(i, (i + s) % planes) for i in range(planes)])

    norm, pieces_of = None, {}
    for group in range(groups):
        span = range(1, planes)
        result, norm = attend(norm, [group], span, False, 2.0 * len(span))
        for s, piece in zip(span, result):
            pieces_of[s, group] = send(piece, s)
    (piece,), norm = attend(norm, list(range(groups)), range(1), True, 4.0)
    pieces_of[0, 0] = piece
    block_rows = rows // shards
    served = lax.all_to_all(
        norm.reshape(shards, block_rows, HEAD_DIM), "tok", split_axis=0, concat_axis=0, tiled=True
    ).reshape(rows, HEAD_DIM)
    places = sorted(pieces_of)
    flat = [pieces_of[place] for place in places]
    with jax.named_scope("assemble"):
        attention_out, served_lse = pl.pallas_call(
            partial(assemble_kernel, planes, per_group * HEAD_DIM, groups, places),
            out_shape=[
                jax.ShapeDtypeStruct((tile, planes * heads * HEAD_DIM), jnp.bfloat16),
                jax.ShapeDtypeStruct((heads, rows), jnp.float32),
            ],
            in_specs=[smem(), vmem()] + [hbm()] * len(flat),
            out_specs=[hbm(), hbm()],
            scratch_shapes=[
                pltpu.VMEM((heads, rows), jnp.float32),
                pltpu.SemaphoreType.DMA((len(flat) + 1,)),
            ],
            compiler_params=params(),
        )(where, served, *flat)
    return (attention_out, served_lse)


def solution(mesh):
    return jax.shard_map(
        body,
        mesh=mesh,
        in_specs=(P("tok", "kv"), P("tok", "kv"), P("tok", "kv"), P(), P()),
        out_specs=(P(("tok", "kv"), None), P("kv", "tok")),
        check_vma=False,
    )
```

```python
import math
from functools import partial

import jax
import jax.numpy as jnp
import numpy as np
from jax import lax
from jax.experimental import pallas as pl
from jax.experimental.pallas import tpu as pltpu
from jax.sharding import PartitionSpec as P

HEAD_DIM = 128
HALF = HEAD_DIM // 2
THETA = 500000.0
NEG = -1e30
LOG2E = math.log2(math.e)
SCALE = 1.0 / math.sqrt(HEAD_DIM)
VMEM_LIMIT = 48 * 1024 * 1024


def vmem():
    return pl.BlockSpec(memory_space=pltpu.VMEM)


def smem():
    return pl.BlockSpec(memory_space=pltpu.SMEM)


def hbm():
    return pl.BlockSpec(memory_space=pl.ANY)


def far_hbm():
    return pl.BlockSpec(memory_space=pltpu.HBM)


def params():
    return pltpu.CompilerParams(vmem_limit_bytes=VMEM_LIMIT)


def cost(microseconds):
    return pl.CostEstimate(flops=int(microseconds * 1.15e9), bytes_accessed=0, transcendentals=0)


def doc_starts(lengths_ref, token):
    begin = jnp.int32(0)
    start = jnp.zeros_like(token)
    for doc in range(lengths_ref.shape[0] - 1):
        begin = begin + lengths_ref[doc]
        start = jnp.where(token >= begin, begin, start)
    return start


def rotary_tables(lengths_ref, freq_ref, rows, first):
    token = first + lax.broadcasted_iota(jnp.int32, (rows, HEAD_DIM), 0)
    start = doc_starts(lengths_ref, token)
    position = token - start
    angle = position.astype(jnp.float32) * freq_ref[...]
    lane = lax.broadcasted_iota(jnp.int32, (rows, HEAD_DIM), 1)
    sine = jnp.sin(angle)
    return jnp.cos(angle), jnp.where(lane < HALF, -sine, sine), start


def turn(block, cosine, sine):
    x = block.astype(jnp.float32)
    return (x * cosine + pltpu.roll(x, HALF, 1) * sine).astype(jnp.bfloat16)


def pack(out_ref, key_ref, value_ref, cosine, sine):
    for group in range(key_ref.shape[1] // HEAD_DIM):
        cols = slice(group * HEAD_DIM, (group + 1) * HEAD_DIM)
        place = 2 * group * HEAD_DIM
        out_ref[:, place : place + HEAD_DIM] = turn(key_ref[:, cols], cosine, sine)
        out_ref[:, place + HEAD_DIM : place + 2 * HEAD_DIM] = value_ref[:, cols]


def queries_kernel(pieces, lengths_hbm, freq_hbm, key_hbm, value_hbm, query_hbm, *refs):
    pack_ref, start_ref, table_ref = refs[:3]
    turn_refs = refs[3:-6]
    lengths_ref, freq_ref, key_ref, value_ref, query_ref, sems = refs[-6:]
    copies = [
        pltpu.make_async_copy(key_hbm, key_ref, sems.at[0]),
        pltpu.make_async_copy(value_hbm, value_ref, sems.at[1]),
        pltpu.make_async_copy(query_hbm, query_ref, sems.at[2]),
        pltpu.make_async_copy(lengths_hbm, lengths_ref, sems.at[3]),
        pltpu.make_async_copy(freq_hbm, freq_ref, sems.at[4]),
    ]
    for c in copies[::-1]:
        c.start()
    for c in copies[3:]:
        c.wait()
    rows = query_ref.shape[0]
    shard = lax.axis_index("tok")
    cosine, sine, start = rotary_tables(lengths_ref, freq_ref, rows, shard * rows)
    start_ref[...] = start
    for c in copies[:2]:
        c.wait()
    pack(pack_ref, key_ref, value_ref, cosine, sine)
    for p in range(1, pieces + 1):
        far_cosine, far_sine, _ = rotary_tables(lengths_ref, freq_ref, rows, (shard - 2 * p) * rows)
        table_ref[2 * p - 2] = far_cosine
        table_ref[2 * p - 1] = far_sine
    copies[2].wait()
    tiles, stacked, _ = turn_refs[0].shape
    tile = rows // tiles
    per_group = stacked // tile
    for group, out_ref in enumerate(turn_refs):
        for head in range(per_group):
            cols = pl.ds((group * per_group + head) * HEAD_DIM, HEAD_DIM)
            turned = turn(query_ref[:, cols], cosine, sine)
            for t in range(tiles):
                out_ref[t, head * tile : (head + 1) * tile, :] = turned[t * tile : (t + 1) * tile]


def pack_kernel(pieces, table_ref, own_ref, *refs):
    mine_ref, give_ref = refs[-2:]
    relayed = refs[2 * pieces : -2]
    shard = lax.axis_index("tok")
    mine_ref[0] = own_ref[...]
    for p in range(pieces):
        keys = refs[p][...]
        if relayed and not p:
            keys = jnp.where(shard // 2 == 2, relayed[0][...], keys)
        pack(
            mine_ref.at[p + 1],
            keys,
            refs[pieces + p][...],
            table_ref[2 * p],
            table_ref[2 * p + 1],
        )
    odd = lax.rem(shard, 2)
    for p in range(pieces):
        give_ref[p] = mine_ref[p + odd]


def attend_kernel(pieces, per_group, groups, tiles_of, begun, last, *refs):
    norm_ref = None
    if last:
        plan_hbm, refs = refs[0], refs[1:]
        plan_ref, plan_sem = refs[-2:]
        refs = refs[:-2]
        plan_copy = pltpu.make_async_copy(plan_hbm, plan_ref, plan_sem.at[0])
        plan_copy.start()
    start_ref, refs = refs[0], refs[1:]
    if begun:
        norm_ref, refs = refs[0], refs[1:]
    slots = 2 * pieces + 1
    tasks = len(tiles_of)
    mine_ref, theirs_ref = refs[:2]
    refs = refs[2:]
    query_refs, refs = dict(zip(groups, refs)), refs[len(groups) :]
    out_refs, lse_ref = refs[:tasks], refs[tasks]
    staged, norms = refs[tasks + 1 :]
    shard, z = lax.axis_index("tok"), lax.axis_index("kv")
    tiles, stacked, _ = query_refs[groups[0]].shape
    tile = stacked // per_group
    rows = tile * tiles
    def window(group, slot, part):
        place = (2 * group + part) * HEAD_DIM
        cols = slice(place, place + HEAD_DIM)
        back = slots - 1 - slot
        if back % 2 == 0:
            return mine_ref[back // 2, :, cols]
        return theirs_ref[back // 2, :, cols]

    first = shard * rows
    window_first = (shard - (slots - 1)) * rows
    exponent = SCALE * LOG2E
    column = lax.broadcasted_iota(jnp.int32, (tile, HEAD_DIM), 1)
    line = lax.broadcasted_iota(jnp.int32, (tile, HEAD_DIM), 0)
    chunk = min(stacked, 256)
    inside = chunk // tile
    norms[...] = norm_ref[...] if begun else jnp.zeros(norms.shape, jnp.float32)

    def masks_of(t):
        start = start_ref[pl.ds(pl.multiple_of(t * tile, tile), tile), :]
        masks = []
        for slot in range(slots):
            begins = start - (window_first + slot * rows)
            for lane in range(0, rows, HEAD_DIM):
                allowed = column + lane >= begins
                if slot == slots - 1:
                    allowed = allowed & (column + lane <= line + t * tile)
                masks.append(allowed[None])
        return masks

    def scores_of(group, t, c, masks):
        q = query_refs[group][t, c * chunk : (c + 1) * chunk, :]
        parts, best = [], None
        for slot in range(slots):
            block = lax.dot_general(
                q,
                window(group, slot, 0),
                (((1,), (1,)), ((), ())),
                preferred_element_type=jnp.float32,
            )
            for lane in range(0, rows, HEAD_DIM):
                part = block[:, lane : lane + HEAD_DIM].reshape(inside, tile, HEAD_DIM)
                part = jnp.where(masks[len(parts)], part, NEG).reshape(chunk, HEAD_DIM)
                parts.append(part)
                best = part if best is None else jnp.maximum(best, part)
        return parts, best

    def mix(index, c, i, parts, best, gathered):
        group = groups[index]
        top = jnp.max(best, axis=1, keepdims=True) * exponent
        total, mixed = None, None
        per_slot = rows // HEAD_DIM
        for slot in range(slots):
            probs = []
            for part in parts[per_slot * slot : per_slot * (slot + 1)]:
                weights = jnp.exp2(part * exponent - top)
                total = weights if total is None else total + weights
                probs.append(weights.astype(jnp.bfloat16))
            product = jnp.dot(
                jnp.concatenate(probs, axis=1),
                window(group, slot, 1),
                preferred_element_type=jnp.float32,
            )
            mixed = product if mixed is None else mixed + product
        row_sum = jnp.sum(total, axis=1, keepdims=True)
        result = (mixed / row_sum).astype(jnp.bfloat16)
        norm = top * (1.0 / LOG2E) + jnp.log(row_sum)
        for h in range(inside):
            head = c * inside + h
            part = slice(h * tile, (h + 1) * tile)
            column_of = (index * per_group + head) * HEAD_DIM
            staged[i, :, column_of : column_of + HEAD_DIM] = result[part]
            gathered = jnp.where(column == group * per_group + head, norm[part], gathered)
        return gathered

    def step(i, carry):
        t = lax.rem(z + tiles_of.start + i * tiles_of.step, tiles)
        here = pl.ds(pl.multiple_of(t * tile, tile), tile)
        gathered = norms[here, :]
        masks = masks_of(t)
        jobs = [(index, c) for index in range(len(groups)) for c in range(stacked // chunk)]
        ready = scores_of(groups[0], t, 0, masks)
        for job, (index, c) in enumerate(jobs):
            following = None
            if job + 1 < len(jobs):
                next_index, next_c = jobs[job + 1]
                following = scores_of(groups[next_index], t, next_c, masks)
            gathered = mix(index, c, i, *ready, gathered)
            ready = following
        norms[here, :] = gathered
        return carry

    lax.fori_loop(0, len(tiles_of), step, 0, unroll=slots <= 5)

    for position, out_ref in enumerate(out_refs):
        out_ref[...] = staged[position]
    if last:
        plan_copy.wait()
        shards = plan_ref.shape[0]
        block = rows // shards
        for s in range(shards):
            picked = pl.multiple_of(plan_ref[shard, s] * block, block)
            lse_ref[s * block : (s + 1) * block, :] = norms[pl.ds(picked, block), :]
    else:
        lse_ref[...] = norms[...]


def assemble_kernel(planes, width, groups, places, served_ref, *refs):
    pieces, out_ref, lse_hbm, lse_ref, sems = refs[:-4], *refs[-4:]
    z = lax.axis_index("kv")
    copies = []
    for index, (s, group) in enumerate(places):
        origin = lax.rem(z - s + planes, planes)
        column = pl.multiple_of((origin * groups + group) * width, width)
        target = out_ref.at[:, pl.ds(column, pieces[index].shape[1])]
        copies.append(pltpu.make_async_copy(pieces[index], target, sems.at[index]))
    for c in copies:
        c.start()
    lse_ref[...] = served_ref[...].T[: lse_ref.shape[0]]
    lse_copy = pltpu.make_async_copy(lse_ref, lse_hbm, sems.at[len(pieces)])
    lse_copy.start()
    for c in copies:
        c.wait()
    lse_copy.wait()


def body(queries, key_states, value_states, doc_lengths, block_plan):
    shards = lax.axis_size("tok")
    planes = lax.axis_size("kv")
    rows = queries.shape[0]
    groups = key_states.shape[1] // HEAD_DIM
    heads = queries.shape[1] // HEAD_DIM
    per_group = heads // groups
    tile = rows // planes
    pieces = shards // 4
    half_freq = THETA ** (-np.arange(HALF, dtype=np.float64) * 2.0 / HEAD_DIM)
    freq = jnp.asarray(np.concatenate([half_freq, half_freq])[None, :], jnp.float32)

    pair = [(i, i ^ 1) for i in range(shards)]

    def forward(x, p):
        return lax.ppermute(x, "tok", [(i, i + 2 * p) for i in range(shards - 2 * p)])

    far_keys = [forward(key_states, p) for p in range(1, pieces + 1)]
    far_values = [forward(value_states, p) for p in range(1, pieces + 1)]
    relayed = []
    after = queries
    if shards == 8:
        far_keys[0] = lax.ppermute(key_states, "tok", [(0, 2), (1, 3), (4, 6), (5, 7)])
        relayed = [lax.ppermute(far_keys[1], "tok", [(6, 4), (7, 5)])]
        after, _ = lax.optimization_barrier((queries, far_keys[1]))
    pack_shape = jax.ShapeDtypeStruct((rows, 2 * groups * HEAD_DIM), jnp.bfloat16)
    with jax.named_scope("rotate"):
        result = pl.pallas_call(
            partial(queries_kernel, pieces),
            out_shape=[
                pack_shape,
                jax.ShapeDtypeStruct((rows, HEAD_DIM), jnp.int32),
                jax.ShapeDtypeStruct((2 * pieces, rows, HEAD_DIM), jnp.float32),
            ]
            + [jax.ShapeDtypeStruct((planes, per_group * tile, HEAD_DIM), jnp.bfloat16)] * groups,
            in_specs=[hbm()] * 5,
            out_specs=[vmem()] * (3 + groups),
            scratch_shapes=[
                pltpu.SMEM(doc_lengths.shape, jnp.int32),
                pltpu.VMEM(freq.shape, jnp.float32),
                pltpu.VMEM(key_states.shape, jnp.bfloat16),
                pltpu.VMEM(value_states.shape, jnp.bfloat16),
                pltpu.VMEM(queries.shape, jnp.bfloat16),
                pltpu.SemaphoreType.DMA((5,)),
            ],
            compiler_params=params(),
            cost_estimate=cost(3.0),
        )(
            pltpu.with_memory_space_constraint(doc_lengths, pltpu.HBM),
            pltpu.with_memory_space_constraint(freq, pltpu.HBM),
            pltpu.with_memory_space_constraint(key_states, pltpu.HBM),
            pltpu.with_memory_space_constraint(value_states, pltpu.HBM),
            pltpu.with_memory_space_constraint(after, pltpu.HBM),
        )
    own, start, tables = result[:3]
    turned = result[3:]
    with jax.named_scope("pack"):
        mine, give = pl.pallas_call(
            partial(pack_kernel, pieces),
            out_shape=[
                jax.ShapeDtypeStruct((count, *pack_shape.shape), jnp.bfloat16)
                for count in (pieces + 1, pieces)
            ],
            in_specs=[vmem()] * (2 + 2 * pieces + len(relayed)),
            out_specs=[vmem()] * 2,
            compiler_params=params(),
            cost_estimate=cost(1.0),
        )(tables, own, *far_keys, *far_values, *relayed)
    theirs = lax.ppermute(give, "tok", pair)

    def attend(norm, used, tiles_of, last, microseconds):
        plan = [pltpu.with_memory_space_constraint(block_plan, pltpu.HBM)] if last else []
        operands = [start] if norm is None else [start, norm]
        operands += [mine, theirs] + [turned[group] for group in used]
        tasks = len(tiles_of)
        width = len(used) * per_group * HEAD_DIM
        with jax.named_scope("attend"):
            result = pl.pallas_call(
                partial(
                    attend_kernel, pieces, per_group, used, tiles_of, norm is not None, last
                ),
                out_shape=[jax.ShapeDtypeStruct((tile, width), jnp.bfloat16)]
                * tasks
                + [jax.ShapeDtypeStruct((rows, HEAD_DIM), jnp.float32)],
                in_specs=[hbm()] * len(plan) + [vmem()] * len(operands),
                out_specs=[vmem()] * (tasks + 1),
                scratch_shapes=[
                    pltpu.VMEM((tasks, tile, width), jnp.bfloat16),
                    pltpu.VMEM((rows, HEAD_DIM), jnp.float32),
                ]
                + [pltpu.SMEM(block_plan.shape, jnp.int32), pltpu.SemaphoreType.DMA((1,))]
                * len(plan),
                compiler_params=params(),
                cost_estimate=cost(microseconds),
            )(*plan, *operands)
        return result[:tasks], result[tasks]

    def send(piece, s):
        return lax.ppermute(piece, "kv", [(i, (i + s) % planes) for i in range(planes)])

    norm, pieces_of = None, {}
    for group in range(groups):
        spans = [range(1, planes)]
        for span in spans:
            result, norm = attend(norm, [group], span, False, 0.01)
            for s, piece in zip(span, result):
                pieces_of[s, group] = send(piece, s)
    (piece,), norm = attend(norm, list(range(groups)), range(1), True, 4.0)
    pieces_of[0, 0] = piece
    block_rows = rows // shards
    served = lax.all_to_all(
        norm.reshape(shards, block_rows, HEAD_DIM), "tok", split_axis=0, concat_axis=0, tiled=True
    ).reshape(rows, HEAD_DIM)
    places = sorted(pieces_of)
    flat = [pieces_of[place] for place in places]
    with jax.named_scope("assemble"):
        attention_out, served_lse = pl.pallas_call(
            partial(assemble_kernel, planes, per_group * HEAD_DIM, groups, places),
            out_shape=[
                jax.ShapeDtypeStruct((tile, planes * heads * HEAD_DIM), jnp.bfloat16),
                jax.ShapeDtypeStruct((heads, rows), jnp.float32),
            ],
            in_specs=[vmem()] + [hbm()] * len(flat),
            out_specs=[hbm(), hbm()],
            scratch_shapes=[
                pltpu.VMEM((heads, rows), jnp.float32),
                pltpu.SemaphoreType.DMA((len(flat) + 1,)),
            ],
            compiler_params=params(),
        )(served, *flat)
    return (attention_out, served_lse)


def solution(mesh):
    return jax.shard_map(
        body,
        mesh=mesh,
        in_specs=(P("tok", "kv"), P("tok", "kv"), P("tok", "kv"), P(), P()),
        out_specs=(P(("tok", "kv"), None), P("kv", "tok")),
        check_vma=False,
    )
```

```python
import math
from functools import partial

import jax
import jax.numpy as jnp
import numpy as np
from jax import lax
from jax.experimental import pallas as pl
from jax.experimental.pallas import tpu as pltpu
from jax.sharding import PartitionSpec as P

HEAD_DIM = 128
HALF = HEAD_DIM // 2
THETA = 500000.0
NEG = -1e30
LOG2E = math.log2(math.e)
SCALE = 1.0 / math.sqrt(HEAD_DIM)
VMEM_LIMIT = 48 * 1024 * 1024


def vmem():
    return pl.BlockSpec(memory_space=pltpu.VMEM)


def smem():
    return pl.BlockSpec(memory_space=pltpu.SMEM)


def hbm():
    return pl.BlockSpec(memory_space=pl.ANY)


def far_hbm():
    return pl.BlockSpec(memory_space=pltpu.HBM)


def params():
    return pltpu.CompilerParams(vmem_limit_bytes=VMEM_LIMIT)


def cost(microseconds):
    return pl.CostEstimate(flops=int(microseconds * 1.15e9), bytes_accessed=0, transcendentals=0)


def doc_starts(lengths_ref, token):
    begin = jnp.int32(0)
    start = jnp.zeros_like(token)
    for doc in range(lengths_ref.shape[0] - 1):
        begin = begin + lengths_ref[doc]
        start = jnp.where(token >= begin, begin, start)
    return start


def rotary_tables(lengths_ref, freq_ref, rows, first):
    token = first + lax.broadcasted_iota(jnp.int32, (rows, HEAD_DIM), 0)
    start = doc_starts(lengths_ref, token)
    position = token - start
    angle = position.astype(jnp.float32) * freq_ref[...]
    lane = lax.broadcasted_iota(jnp.int32, (rows, HEAD_DIM), 1)
    sine = jnp.sin(angle)
    return jnp.cos(angle), jnp.where(lane < HALF, -sine, sine), start


def turn(block, cosine, sine):
    x = block.astype(jnp.float32)
    return (x * cosine + pltpu.roll(x, HALF, 1) * sine).astype(jnp.bfloat16)


def pack(out_ref, key_ref, value_ref, cosine, sine):
    for group in range(key_ref.shape[1] // HEAD_DIM):
        cols = slice(group * HEAD_DIM, (group + 1) * HEAD_DIM)
        place = 2 * group * HEAD_DIM
        out_ref[:, place : place + HEAD_DIM] = turn(key_ref[:, cols], cosine, sine)
        out_ref[:, place + HEAD_DIM : place + 2 * HEAD_DIM] = value_ref[:, cols]


def queries_kernel(pieces, lengths_hbm, freq_hbm, key_hbm, value_hbm, query_hbm, *refs):
    pack_ref, start_ref, table_ref = refs[:3]
    turn_refs = refs[3:-6]
    lengths_ref, freq_ref, key_ref, value_ref, query_ref, sems = refs[-6:]
    copies = [
        pltpu.make_async_copy(key_hbm, key_ref, sems.at[0]),
        pltpu.make_async_copy(value_hbm, value_ref, sems.at[1]),
        pltpu.make_async_copy(query_hbm, query_ref, sems.at[2]),
        pltpu.make_async_copy(lengths_hbm, lengths_ref, sems.at[3]),
        pltpu.make_async_copy(freq_hbm, freq_ref, sems.at[4]),
    ]
    for c in copies[::-1]:
        c.start()
    for c in copies[3:]:
        c.wait()
    rows = query_ref.shape[0]
    shard = lax.axis_index("tok")
    cosine, sine, start = rotary_tables(lengths_ref, freq_ref, rows, shard * rows)
    start_ref[...] = start
    for c in copies[:2]:
        c.wait()
    pack(pack_ref, key_ref, value_ref, cosine, sine)
    for p in range(1, pieces + 1):
        far_cosine, far_sine, _ = rotary_tables(lengths_ref, freq_ref, rows, (shard - 2 * p) * rows)
        table_ref[2 * p - 2] = far_cosine
        table_ref[2 * p - 1] = far_sine
    copies[2].wait()
    tiles, stacked, _ = turn_refs[0].shape
    tile = rows // tiles
    per_group = stacked // tile
    for group, out_ref in enumerate(turn_refs):
        for head in range(per_group):
            cols = pl.ds((group * per_group + head) * HEAD_DIM, HEAD_DIM)
            turned = turn(query_ref[:, cols], cosine, sine)
            for t in range(tiles):
                out_ref[t, head * tile : (head + 1) * tile, :] = turned[t * tile : (t + 1) * tile]


def pack_kernel(pieces, table_ref, own_ref, *refs):
    mine_ref, give_ref = refs[-2:]
    relayed = refs[2 * pieces : -2]
    shard = lax.axis_index("tok")
    mine_ref[0] = own_ref[...]
    for p in range(pieces):
        keys = refs[p][...]
        if relayed and not p:
            keys = jnp.where(shard // 2 == 2, relayed[0][...], keys)
        pack(
            mine_ref.at[p + 1],
            keys,
            refs[pieces + p][...],
            table_ref[2 * p],
            table_ref[2 * p + 1],
        )
    odd = lax.rem(shard, 2)
    for p in range(pieces):
        give_ref[p] = mine_ref[p + odd]


def attend_kernel(pieces, per_group, groups, tiles_of, begun, last, *refs):
    norm_ref = None
    if last:
        plan_hbm, refs = refs[0], refs[1:]
        plan_ref, plan_sem = refs[-2:]
        refs = refs[:-2]
        plan_copy = pltpu.make_async_copy(plan_hbm, plan_ref, plan_sem.at[0])
        plan_copy.start()
    start_ref, refs = refs[0], refs[1:]
    if begun:
        norm_ref, refs = refs[0], refs[1:]
    slots = 2 * pieces + 1
    tasks = len(tiles_of)
    mine_ref, theirs_ref = refs[:2]
    refs = refs[2:]
    query_refs, refs = dict(zip(groups, refs)), refs[len(groups) :]
    out_refs, lse_ref = refs[:tasks], refs[tasks]
    staged, norms = refs[tasks + 1 :]
    shard, z = lax.axis_index("tok"), lax.axis_index("kv")
    tiles, stacked, _ = query_refs[groups[0]].shape
    tile = stacked // per_group
    rows = tile * tiles
    def window(group, slot, part):
        place = (2 * group + part) * HEAD_DIM
        cols = slice(place, place + HEAD_DIM)
        back = slots - 1 - slot
        if back % 2 == 0:
            return mine_ref[back // 2, :, cols]
        return theirs_ref[back // 2, :, cols]

    first = shard * rows
    window_first = (shard - (slots - 1)) * rows
    exponent = SCALE * LOG2E
    column = lax.broadcasted_iota(jnp.int32, (tile, HEAD_DIM), 1)
    line = lax.broadcasted_iota(jnp.int32, (tile, HEAD_DIM), 0)
    chunk = min(stacked, 256)
    inside = chunk // tile
    norms[...] = norm_ref[...] if begun else jnp.zeros(norms.shape, jnp.float32)

    def masks_of(t):
        start = start_ref[pl.ds(pl.multiple_of(t * tile, tile), tile), :]
        masks = []
        for slot in range(slots):
            begins = start - (window_first + slot * rows)
            for lane in range(0, rows, HEAD_DIM):
                allowed = column + lane >= begins
                if slot == slots - 1:
                    allowed = allowed & (column + lane <= line + t * tile)
                masks.append(allowed[None])
        return masks

    def scores_of(group, t, c, masks):
        q = query_refs[group][t, c * chunk : (c + 1) * chunk, :]
        parts, best = [], None
        for slot in range(slots):
            block = lax.dot_general(
                q,
                window(group, slot, 0),
                (((1,), (1,)), ((), ())),
                preferred_element_type=jnp.float32,
            )
            for lane in range(0, rows, HEAD_DIM):
                part = block[:, lane : lane + HEAD_DIM].reshape(inside, tile, HEAD_DIM)
                part = jnp.where(masks[len(parts)], part, NEG).reshape(chunk, HEAD_DIM)
                parts.append(part)
                best = part if best is None else jnp.maximum(best, part)
        return parts, best

    def mix(index, c, i, parts, best, gathered):
        group = groups[index]
        top = jnp.max(best, axis=1, keepdims=True) * exponent
        total, mixed = None, None
        per_slot = rows // HEAD_DIM
        for slot in range(slots):
            probs = []
            for part in parts[per_slot * slot : per_slot * (slot + 1)]:
                weights = jnp.exp2(part * exponent - top)
                total = weights if total is None else total + weights
                probs.append(weights.astype(jnp.bfloat16))
            product = jnp.dot(
                jnp.concatenate(probs, axis=1),
                window(group, slot, 1),
                preferred_element_type=jnp.float32,
            )
            mixed = product if mixed is None else mixed + product
        row_sum = jnp.sum(total, axis=1, keepdims=True)
        result = (mixed / row_sum).astype(jnp.bfloat16)
        norm = top * (1.0 / LOG2E) + jnp.log(row_sum)
        for h in range(inside):
            head = c * inside + h
            part = slice(h * tile, (h + 1) * tile)
            column_of = (index * per_group + head) * HEAD_DIM
            staged[i, :, column_of : column_of + HEAD_DIM] = result[part]
            gathered = jnp.where(column == group * per_group + head, norm[part], gathered)
        return gathered

    def step(i, carry):
        t = lax.rem(z + tiles_of.start + i * tiles_of.step, tiles)
        here = pl.ds(pl.multiple_of(t * tile, tile), tile)
        gathered = norms[here, :]
        masks = masks_of(t)
        jobs = [(index, c) for index in range(len(groups)) for c in range(stacked // chunk)]
        ready = scores_of(groups[0], t, 0, masks)
        for job, (index, c) in enumerate(jobs):
            following = None
            if job + 1 < len(jobs):
                next_index, next_c = jobs[job + 1]
                following = scores_of(groups[next_index], t, next_c, masks)
            gathered = mix(index, c, i, *ready, gathered)
            ready = following
        norms[here, :] = gathered
        return carry

    lax.fori_loop(0, len(tiles_of), step, 0, unroll=slots <= 5)

    for position, out_ref in enumerate(out_refs):
        out_ref[...] = staged[position]
    if last:
        plan_copy.wait()
        shards = plan_ref.shape[0]
        block = rows // shards
        for s in range(shards):
            picked = pl.multiple_of(plan_ref[shard, s] * block, block)
            lse_ref[s * block : (s + 1) * block, :] = norms[pl.ds(picked, block), :]
    else:
        lse_ref[...] = norms[...]


def assemble_kernel(planes, width, groups, places, served_ref, *refs):
    pieces, out_ref, lse_hbm, lse_ref, sems = refs[:-4], *refs[-4:]
    z = lax.axis_index("kv")
    copies = []
    for index, (s, group) in enumerate(places):
        origin = lax.rem(z - s + planes, planes)
        column = pl.multiple_of((origin * groups + group) * width, width)
        target = out_ref.at[:, pl.ds(column, pieces[index].shape[1])]
        copies.append(pltpu.make_async_copy(pieces[index], target, sems.at[index]))
    for c in copies:
        c.start()
    lse_ref[...] = served_ref[...].T[: lse_ref.shape[0]]
    lse_copy = pltpu.make_async_copy(lse_ref, lse_hbm, sems.at[len(pieces)])
    lse_copy.start()
    for c in copies:
        c.wait()
    lse_copy.wait()


def body(queries, key_states, value_states, doc_lengths, block_plan):
    shards = lax.axis_size("tok")
    planes = lax.axis_size("kv")
    rows = queries.shape[0]
    groups = key_states.shape[1] // HEAD_DIM
    heads = queries.shape[1] // HEAD_DIM
    per_group = heads // groups
    tile = rows // planes
    pieces = shards // 4
    half_freq = THETA ** (-np.arange(HALF, dtype=np.float64) * 2.0 / HEAD_DIM)
    freq = jnp.asarray(np.concatenate([half_freq, half_freq])[None, :], jnp.float32)

    pair = [(i, i ^ 1) for i in range(shards)]

    def forward(x, p):
        return lax.ppermute(x, "tok", [(i, i + 2 * p) for i in range(shards - 2 * p)])

    far_keys = [forward(key_states, p) for p in range(1, pieces + 1)]
    far_values = [forward(value_states, p) for p in range(1, pieces + 1)]
    relayed = []
    after = queries
    if shards == 8:
        far_keys[0] = lax.ppermute(key_states, "tok", [(0, 2), (1, 3), (4, 6), (5, 7)])
        relayed = [lax.ppermute(far_keys[1], "tok", [(6, 4), (7, 5)])]
        after, _ = lax.optimization_barrier((queries, far_keys[1]))
    pack_shape = jax.ShapeDtypeStruct((rows, 2 * groups * HEAD_DIM), jnp.bfloat16)
    with jax.named_scope("rotate"):
        result = pl.pallas_call(
            partial(queries_kernel, pieces),
            out_shape=[
                pack_shape,
                jax.ShapeDtypeStruct((rows, HEAD_DIM), jnp.int32),
                jax.ShapeDtypeStruct((2 * pieces, rows, HEAD_DIM), jnp.float32),
            ]
            + [jax.ShapeDtypeStruct((planes, per_group * tile, HEAD_DIM), jnp.bfloat16)] * groups,
            in_specs=[hbm()] * 5,
            out_specs=[vmem()] * (3 + groups),
            scratch_shapes=[
                pltpu.SMEM(doc_lengths.shape, jnp.int32),
                pltpu.VMEM(freq.shape, jnp.float32),
                pltpu.VMEM(key_states.shape, jnp.bfloat16),
                pltpu.VMEM(value_states.shape, jnp.bfloat16),
                pltpu.VMEM(queries.shape, jnp.bfloat16),
                pltpu.SemaphoreType.DMA((5,)),
            ],
            compiler_params=params(),
            cost_estimate=cost(3.0),
        )(
            pltpu.with_memory_space_constraint(doc_lengths, pltpu.HBM),
            pltpu.with_memory_space_constraint(freq, pltpu.HBM),
            pltpu.with_memory_space_constraint(key_states, pltpu.HBM),
            pltpu.with_memory_space_constraint(value_states, pltpu.HBM),
            pltpu.with_memory_space_constraint(after, pltpu.HBM),
        )
    own, start, tables = result[:3]
    turned = result[3:]
    with jax.named_scope("pack"):
        mine, give = pl.pallas_call(
            partial(pack_kernel, pieces),
            out_shape=[
                jax.ShapeDtypeStruct((count, *pack_shape.shape), jnp.bfloat16)
                for count in (pieces + 1, pieces)
            ],
            in_specs=[vmem()] * (2 + 2 * pieces + len(relayed)),
            out_specs=[vmem()] * 2,
            compiler_params=params(),
            cost_estimate=cost(1.0),
        )(tables, own, *far_keys, *far_values, *relayed)
    theirs = lax.ppermute(give, "tok", pair)

    def attend(norm, used, tiles_of, last, microseconds):
        plan = [pltpu.with_memory_space_constraint(block_plan, pltpu.HBM)] if last else []
        operands = [start] if norm is None else [start, norm]
        operands += [mine, theirs] + [turned[group] for group in used]
        tasks = len(tiles_of)
        width = len(used) * per_group * HEAD_DIM
        with jax.named_scope("attend"):
            result = pl.pallas_call(
                partial(
                    attend_kernel, pieces, per_group, used, tiles_of, norm is not None, last
                ),
                out_shape=[jax.ShapeDtypeStruct((tile, width), jnp.bfloat16)]
                * tasks
                + [jax.ShapeDtypeStruct((rows, HEAD_DIM), jnp.float32)],
                in_specs=[hbm()] * len(plan) + [vmem()] * len(operands),
                out_specs=[vmem()] * (tasks + 1),
                scratch_shapes=[
                    pltpu.VMEM((tasks, tile, width), jnp.bfloat16),
                    pltpu.VMEM((rows, HEAD_DIM), jnp.float32),
                ]
                + [pltpu.SMEM(block_plan.shape, jnp.int32), pltpu.SemaphoreType.DMA((1,))]
                * len(plan),
                compiler_params=params(),
                cost_estimate=cost(microseconds),
            )(*plan, *operands)
        return result[:tasks], result[tasks]

    def send(piece, s):
        return lax.ppermute(piece, "kv", [(i, (i + s) % planes) for i in range(planes)])

    norm, pieces_of = None, {}
    middle, both = planes // 2, list(range(groups))
    spans = [range(middle, middle + 1), range(1, planes, 2)]
    spans += [range(s, s + 1) for s in range(2, planes, 2) if s != middle]
    for used in [both]:
        (piece,), norm = attend(norm, used, spans[0], False, 2.0 * len(used))
        pieces_of[middle, used[0]] = send(piece, middle)
    for span in spans[1:]:
        result, norm = attend(norm, both, span, False, 4.0 * len(span))
        for s, piece in zip(span, result):
            pieces_of[s, 0] = send(piece, s)
    (piece,), norm = attend(norm, both, range(1), True, 4.0)
    pieces_of[0, 0] = piece
    block_rows = rows // shards
    served = lax.all_to_all(
        norm.reshape(shards, block_rows, HEAD_DIM), "tok", split_axis=0, concat_axis=0, tiled=True
    ).reshape(rows, HEAD_DIM)
    places = sorted(pieces_of)
    flat = [pieces_of[place] for place in places]
    with jax.named_scope("assemble"):
        attention_out, served_lse = pl.pallas_call(
            partial(assemble_kernel, planes, per_group * HEAD_DIM, groups, places),
            out_shape=[
                jax.ShapeDtypeStruct((tile, planes * heads * HEAD_DIM), jnp.bfloat16),
                jax.ShapeDtypeStruct((heads, rows), jnp.float32),
            ],
            in_specs=[vmem()] + [hbm()] * len(flat),
            out_specs=[hbm(), hbm()],
            scratch_shapes=[
                pltpu.VMEM((heads, rows), jnp.float32),
                pltpu.SemaphoreType.DMA((len(flat) + 1,)),
            ],
            compiler_params=params(),
        )(served, *flat)
    return (attention_out, served_lse)


def solution(mesh):
    return jax.shard_map(
        body,
        mesh=mesh,
        in_specs=(P("tok", "kv"), P("tok", "kv"), P("tok", "kv"), P(), P()),
        out_specs=(P(("tok", "kv"), None), P("kv", "tok")),
        check_vma=False,
    )
```

```python
import math
from functools import partial

import jax
import jax.numpy as jnp
import numpy as np
from jax import lax
from jax.experimental import pallas as pl
from jax.experimental.pallas import tpu as pltpu
from jax.sharding import PartitionSpec as P

HEAD_DIM = 128
HALF = HEAD_DIM // 2
THETA = 500000.0
NEG = -1e30
LOG2E = math.log2(math.e)
SCALE = 1.0 / math.sqrt(HEAD_DIM)
VMEM_LIMIT = 48 * 1024 * 1024


def vmem():
    return pl.BlockSpec(memory_space=pltpu.VMEM)


def smem():
    return pl.BlockSpec(memory_space=pltpu.SMEM)


def hbm():
    return pl.BlockSpec(memory_space=pl.ANY)


def far_hbm():
    return pl.BlockSpec(memory_space=pltpu.HBM)


def params():
    return pltpu.CompilerParams(vmem_limit_bytes=VMEM_LIMIT)


def cost(microseconds):
    return pl.CostEstimate(flops=int(microseconds * 1.15e9), bytes_accessed=0, transcendentals=0)


def doc_starts(lengths_ref, token):
    begin = jnp.int32(0)
    start = jnp.zeros_like(token)
    for doc in range(lengths_ref.shape[0] - 1):
        begin = begin + lengths_ref[doc]
        start = jnp.where(token >= begin, begin, start)
    return start


def rotary_tables(lengths_ref, freq_ref, rows, first):
    token = first + lax.broadcasted_iota(jnp.int32, (rows, HEAD_DIM), 0)
    start = doc_starts(lengths_ref, token)
    position = token - start
    angle = position.astype(jnp.float32) * freq_ref[...]
    lane = lax.broadcasted_iota(jnp.int32, (rows, HEAD_DIM), 1)
    sine = jnp.sin(angle)
    return jnp.cos(angle), jnp.where(lane < HALF, -sine, sine), start


def turn(block, cosine, sine):
    x = block.astype(jnp.float32)
    return (x * cosine + pltpu.roll(x, HALF, 1) * sine).astype(jnp.bfloat16)


def pack(out_ref, key_ref, value_ref, cosine, sine):
    for group in range(key_ref.shape[1] // HEAD_DIM):
        cols = slice(group * HEAD_DIM, (group + 1) * HEAD_DIM)
        place = 2 * group * HEAD_DIM
        out_ref[:, place : place + HEAD_DIM] = turn(key_ref[:, cols], cosine, sine)
        out_ref[:, place + HEAD_DIM : place + 2 * HEAD_DIM] = value_ref[:, cols]


def queries_kernel(pieces, lengths_hbm, freq_hbm, key_hbm, value_hbm, query_hbm, *refs):
    pack_ref, start_ref, table_ref = refs[:3]
    turn_refs = refs[3:-6]
    lengths_ref, freq_ref, key_ref, value_ref, query_ref, sems = refs[-6:]
    copies = [
        pltpu.make_async_copy(key_hbm, key_ref, sems.at[0]),
        pltpu.make_async_copy(value_hbm, value_ref, sems.at[1]),
        pltpu.make_async_copy(query_hbm, query_ref, sems.at[2]),
        pltpu.make_async_copy(lengths_hbm, lengths_ref, sems.at[3]),
        pltpu.make_async_copy(freq_hbm, freq_ref, sems.at[4]),
    ]
    for c in copies[::-1]:
        c.start()
    for c in copies[3:]:
        c.wait()
    rows = query_ref.shape[0]
    shard = lax.axis_index("tok")
    cosine, sine, start = rotary_tables(lengths_ref, freq_ref, rows, shard * rows)
    start_ref[...] = start
    for c in copies[:2]:
        c.wait()
    pack(pack_ref, key_ref, value_ref, cosine, sine)
    for p in range(1, pieces + 1):
        far_cosine, far_sine, _ = rotary_tables(lengths_ref, freq_ref, rows, (shard - 2 * p) * rows)
        table_ref[2 * p - 2] = far_cosine
        table_ref[2 * p - 1] = far_sine
    copies[2].wait()
    tiles, stacked, _ = turn_refs[0].shape
    tile = rows // tiles
    per_group = stacked // tile
    for group, out_ref in enumerate(turn_refs):
        for head in range(per_group):
            cols = pl.ds((group * per_group + head) * HEAD_DIM, HEAD_DIM)
            turned = turn(query_ref[:, cols], cosine, sine)
            for t in range(tiles):
                out_ref[t, head * tile : (head + 1) * tile, :] = turned[t * tile : (t + 1) * tile]


def pack_kernel(pieces, table_ref, own_ref, *refs):
    mine_ref, give_ref = refs[-2:]
    relayed = refs[2 * pieces : -2]
    shard = lax.axis_index("tok")
    mine_ref[0] = own_ref[...]
    for p in range(pieces):
        keys = refs[p][...]
        if relayed and not p:
            keys = jnp.where(shard // 2 == 2, relayed[0][...], keys)
        pack(
            mine_ref.at[p + 1],
            keys,
            refs[pieces + p][...],
            table_ref[2 * p],
            table_ref[2 * p + 1],
        )
    odd = lax.rem(shard, 2)
    for p in range(pieces):
        give_ref[p] = mine_ref[p + odd]


def attend_kernel(pieces, per_group, groups, tiles_of, begun, last, *refs):
    norm_ref = None
    if last:
        plan_hbm, refs = refs[0], refs[1:]
        plan_ref, plan_sem = refs[-2:]
        refs = refs[:-2]
        plan_copy = pltpu.make_async_copy(plan_hbm, plan_ref, plan_sem.at[0])
        plan_copy.start()
    start_ref, refs = refs[0], refs[1:]
    if begun:
        norm_ref, refs = refs[0], refs[1:]
    slots = 2 * pieces + 1
    tasks = len(tiles_of)
    mine_ref, theirs_ref = refs[:2]
    refs = refs[2:]
    query_refs, refs = dict(zip(groups, refs)), refs[len(groups) :]
    out_refs, lse_ref = refs[:tasks], refs[tasks]
    staged, norms = refs[tasks + 1 :]
    shard, z = lax.axis_index("tok"), lax.axis_index("kv")
    tiles, stacked, _ = query_refs[groups[0]].shape
    tile = stacked // per_group
    rows = tile * tiles
    def window(group, slot, part):
        place = (2 * group + part) * HEAD_DIM
        cols = slice(place, place + HEAD_DIM)
        back = slots - 1 - slot
        if back % 2 == 0:
            return mine_ref[back // 2, :, cols]
        return theirs_ref[back // 2, :, cols]

    first = shard * rows
    window_first = (shard - (slots - 1)) * rows
    exponent = SCALE * LOG2E
    column = lax.broadcasted_iota(jnp.int32, (tile, HEAD_DIM), 1)
    line = lax.broadcasted_iota(jnp.int32, (tile, HEAD_DIM), 0)
    chunk = min(stacked, 256)
    inside = chunk // tile
    ones = jnp.ones((rows, HEAD_DIM), jnp.bfloat16)
    norms[...] = norm_ref[...] if begun else jnp.zeros(norms.shape, jnp.float32)

    def masks_of(t):
        start = start_ref[pl.ds(pl.multiple_of(t * tile, tile), tile), :]
        masks = []
        for slot in range(slots):
            begins = start - (window_first + slot * rows)
            for lane in range(0, rows, HEAD_DIM):
                allowed = column + lane >= begins
                if slot == slots - 1:
                    allowed = allowed & (column + lane <= line + t * tile)
                masks.append(allowed[None])
        return masks

    def scores_of(group, t, c, masks):
        q = query_refs[group][t, c * chunk : (c + 1) * chunk, :]
        parts, best = [], None
        for slot in range(slots):
            block = lax.dot_general(
                q,
                window(group, slot, 0),
                (((1,), (1,)), ((), ())),
                preferred_element_type=jnp.float32,
            )
            for lane in range(0, rows, HEAD_DIM):
                part = block[:, lane : lane + HEAD_DIM].reshape(inside, tile, HEAD_DIM)
                part = jnp.where(masks[len(parts)], part, NEG).reshape(chunk, HEAD_DIM)
                parts.append(part)
                best = part if best is None else jnp.maximum(best, part)
        return parts, best

    def mix(index, c, i, parts, best, gathered):
        group = groups[index]
        top = jnp.max(best, axis=1, keepdims=True) * exponent
        mixed = None
        per_slot = rows // HEAD_DIM
        for slot in range(slots):
            probs = []
            for part in parts[per_slot * slot : per_slot * (slot + 1)]:
                weights = jnp.exp2(part * exponent - top)
                probs.append(weights.astype(jnp.bfloat16))
            values = jnp.concatenate([window(group, slot, 1), ones], axis=1)
            product = jnp.dot(
                jnp.concatenate(probs, axis=1), values, preferred_element_type=jnp.float32
            )
            mixed = product if mixed is None else mixed + product
        row_sum = mixed[:, HEAD_DIM:]
        result = (mixed[:, :HEAD_DIM] / row_sum).astype(jnp.bfloat16)
        norm = top * (1.0 / LOG2E) + jnp.log(row_sum)
        for h in range(inside):
            head = c * inside + h
            part = slice(h * tile, (h + 1) * tile)
            column_of = (index * per_group + head) * HEAD_DIM
            staged[i, :, column_of : column_of + HEAD_DIM] = result[part]
            gathered = jnp.where(column == group * per_group + head, norm[part], gathered)
        return gathered

    def step(i, carry):
        t = lax.rem(z + tiles_of.start + i * tiles_of.step, tiles)
        here = pl.ds(pl.multiple_of(t * tile, tile), tile)
        gathered = norms[here, :]
        masks = masks_of(t)
        jobs = [(index, c) for index in range(len(groups)) for c in range(stacked // chunk)]
        ready = scores_of(groups[0], t, 0, masks)
        for job, (index, c) in enumerate(jobs):
            following = None
            if job + 1 < len(jobs):
                next_index, next_c = jobs[job + 1]
                following = scores_of(groups[next_index], t, next_c, masks)
            gathered = mix(index, c, i, *ready, gathered)
            ready = following
        norms[here, :] = gathered
        return carry

    lax.fori_loop(0, len(tiles_of), step, 0, unroll=slots <= 5)

    for position, out_ref in enumerate(out_refs):
        out_ref[...] = staged[position]
    if last:
        plan_copy.wait()
        shards = plan_ref.shape[0]
        block = rows // shards
        for s in range(shards):
            picked = pl.multiple_of(plan_ref[shard, s] * block, block)
            lse_ref[s * block : (s + 1) * block, :] = norms[pl.ds(picked, block), :]
    else:
        lse_ref[...] = norms[...]


def assemble_kernel(planes, width, groups, places, served_ref, *refs):
    pieces, out_ref, lse_hbm, lse_ref, sems = refs[:-4], *refs[-4:]
    z = lax.axis_index("kv")
    copies = []
    for index, (s, group) in enumerate(places):
        origin = lax.rem(z - s + planes, planes)
        column = pl.multiple_of((origin * groups + group) * width, width)
        target = out_ref.at[:, pl.ds(column, pieces[index].shape[1])]
        copies.append(pltpu.make_async_copy(pieces[index], target, sems.at[index]))
    for c in copies:
        c.start()
    lse_ref[...] = served_ref[...].T[: lse_ref.shape[0]]
    lse_copy = pltpu.make_async_copy(lse_ref, lse_hbm, sems.at[len(pieces)])
    lse_copy.start()
    for c in copies:
        c.wait()
    lse_copy.wait()


def body(queries, key_states, value_states, doc_lengths, block_plan):
    shards = lax.axis_size("tok")
    planes = lax.axis_size("kv")
    rows = queries.shape[0]
    groups = key_states.shape[1] // HEAD_DIM
    heads = queries.shape[1] // HEAD_DIM
    per_group = heads // groups
    tile = rows // planes
    pieces = shards // 4
    half_freq = THETA ** (-np.arange(HALF, dtype=np.float64) * 2.0 / HEAD_DIM)
    freq = jnp.asarray(np.concatenate([half_freq, half_freq])[None, :], jnp.float32)

    pair = [(i, i ^ 1) for i in range(shards)]

    def forward(x, p):
        return lax.ppermute(x, "tok", [(i, i + 2 * p) for i in range(shards - 2 * p)])

    far_keys = [forward(key_states, p) for p in range(1, pieces + 1)]
    far_values = [forward(value_states, p) for p in range(1, pieces + 1)]
    relayed = []
    after = queries
    if shards == 8:
        far_keys[0] = lax.ppermute(key_states, "tok", [(0, 2), (1, 3), (4, 6), (5, 7)])
        relayed = [lax.ppermute(far_keys[1], "tok", [(6, 4), (7, 5)])]
        after, _ = lax.optimization_barrier((queries, far_keys[1]))
    pack_shape = jax.ShapeDtypeStruct((rows, 2 * groups * HEAD_DIM), jnp.bfloat16)
    with jax.named_scope("rotate"):
        result = pl.pallas_call(
            partial(queries_kernel, pieces),
            out_shape=[
                pack_shape,
                jax.ShapeDtypeStruct((rows, HEAD_DIM), jnp.int32),
                jax.ShapeDtypeStruct((2 * pieces, rows, HEAD_DIM), jnp.float32),
            ]
            + [jax.ShapeDtypeStruct((planes, per_group * tile, HEAD_DIM), jnp.bfloat16)] * groups,
            in_specs=[hbm()] * 5,
            out_specs=[vmem()] * (3 + groups),
            scratch_shapes=[
                pltpu.SMEM(doc_lengths.shape, jnp.int32),
                pltpu.VMEM(freq.shape, jnp.float32),
                pltpu.VMEM(key_states.shape, jnp.bfloat16),
                pltpu.VMEM(value_states.shape, jnp.bfloat16),
                pltpu.VMEM(queries.shape, jnp.bfloat16),
                pltpu.SemaphoreType.DMA((5,)),
            ],
            compiler_params=params(),
            cost_estimate=cost(3.0),
        )(
            pltpu.with_memory_space_constraint(doc_lengths, pltpu.HBM),
            pltpu.with_memory_space_constraint(freq, pltpu.HBM),
            pltpu.with_memory_space_constraint(key_states, pltpu.HBM),
            pltpu.with_memory_space_constraint(value_states, pltpu.HBM),
            pltpu.with_memory_space_constraint(after, pltpu.HBM),
        )
    own, start, tables = result[:3]
    turned = result[3:]
    with jax.named_scope("pack"):
        mine, give = pl.pallas_call(
            partial(pack_kernel, pieces),
            out_shape=[
                jax.ShapeDtypeStruct((count, *pack_shape.shape), jnp.bfloat16)
                for count in (pieces + 1, pieces)
            ],
            in_specs=[vmem()] * (2 + 2 * pieces + len(relayed)),
            out_specs=[vmem()] * 2,
            compiler_params=params(),
            cost_estimate=cost(1.0),
        )(tables, own, *far_keys, *far_values, *relayed)
    theirs = lax.ppermute(give, "tok", pair)

    def attend(norm, used, tiles_of, last, microseconds):
        plan = [pltpu.with_memory_space_constraint(block_plan, pltpu.HBM)] if last else []
        operands = [start] if norm is None else [start, norm]
        operands += [mine, theirs] + [turned[group] for group in used]
        tasks = len(tiles_of)
        width = len(used) * per_group * HEAD_DIM
        with jax.named_scope("attend"):
            result = pl.pallas_call(
                partial(
                    attend_kernel, pieces, per_group, used, tiles_of, norm is not None, last
                ),
                out_shape=[jax.ShapeDtypeStruct((tile, width), jnp.bfloat16)]
                * tasks
                + [jax.ShapeDtypeStruct((rows, HEAD_DIM), jnp.float32)],
                in_specs=[hbm()] * len(plan) + [vmem()] * len(operands),
                out_specs=[vmem()] * (tasks + 1),
                scratch_shapes=[
                    pltpu.VMEM((tasks, tile, width), jnp.bfloat16),
                    pltpu.VMEM((rows, HEAD_DIM), jnp.float32),
                ]
                + [pltpu.SMEM(block_plan.shape, jnp.int32), pltpu.SemaphoreType.DMA((1,))]
                * len(plan),
                compiler_params=params(),
                cost_estimate=cost(microseconds),
            )(*plan, *operands)
        return result[:tasks], result[tasks]

    def send(piece, s):
        return lax.ppermute(piece, "kv", [(i, (i + s) % planes) for i in range(planes)])

    norm, pieces_of = None, {}
    middle, both = planes // 2, list(range(groups))
    spans = [range(middle, middle + 1), range(1, planes, 2)]
    spans += [range(s, s + 1) for s in range(2, planes, 2) if s != middle]
    for used in [both]:
        (piece,), norm = attend(norm, used, spans[0], False, 2.0 * len(used))
        pieces_of[middle, used[0]] = send(piece, middle)
    for span in spans[1:]:
        result, norm = attend(norm, both, span, False, 4.0 * len(span))
        for s, piece in zip(span, result):
            pieces_of[s, 0] = send(piece, s)
    (piece,), norm = attend(norm, both, range(1), True, 4.0)
    pieces_of[0, 0] = piece
    block_rows = rows // shards
    served = lax.all_to_all(
        norm.reshape(shards, block_rows, HEAD_DIM), "tok", split_axis=0, concat_axis=0, tiled=True
    ).reshape(rows, HEAD_DIM)
    places = sorted(pieces_of)
    flat = [pieces_of[place] for place in places]
    with jax.named_scope("assemble"):
        attention_out, served_lse = pl.pallas_call(
            partial(assemble_kernel, planes, per_group * HEAD_DIM, groups, places),
            out_shape=[
                jax.ShapeDtypeStruct((tile, planes * heads * HEAD_DIM), jnp.bfloat16),
                jax.ShapeDtypeStruct((heads, rows), jnp.float32),
            ],
            in_specs=[vmem()] + [hbm()] * len(flat),
            out_specs=[hbm(), hbm()],
            scratch_shapes=[
                pltpu.VMEM((heads, rows), jnp.float32),
                pltpu.SemaphoreType.DMA((len(flat) + 1,)),
            ],
            compiler_params=params(),
        )(served, *flat)
    return (attention_out, served_lse)


def solution(mesh):
    return jax.shard_map(
        body,
        mesh=mesh,
        in_specs=(P("tok", "kv"), P("tok", "kv"), P("tok", "kv"), P(), P()),
        out_specs=(P(("tok", "kv"), None), P("kv", "tok")),
        check_vma=False,
    )
```

```python
import math
from functools import partial

import jax
import jax.numpy as jnp
import numpy as np
from jax import lax
from jax.experimental import pallas as pl
from jax.experimental.pallas import tpu as pltpu
from jax.sharding import PartitionSpec as P

HEAD_DIM = 128
HALF = HEAD_DIM // 2
THETA = 500000.0
NEG = -1e30
LOG2E = math.log2(math.e)
SCALE = 1.0 / math.sqrt(HEAD_DIM)
VMEM_LIMIT = 48 * 1024 * 1024


def vmem():
    return pl.BlockSpec(memory_space=pltpu.VMEM)


def smem():
    return pl.BlockSpec(memory_space=pltpu.SMEM)


def hbm():
    return pl.BlockSpec(memory_space=pl.ANY)


def far_hbm():
    return pl.BlockSpec(memory_space=pltpu.HBM)


def params():
    return pltpu.CompilerParams(vmem_limit_bytes=VMEM_LIMIT)


def cost(microseconds):
    return pl.CostEstimate(flops=int(microseconds * 1.15e9), bytes_accessed=0, transcendentals=0)


def doc_starts(lengths_ref, token):
    begin = jnp.int32(0)
    start = jnp.zeros_like(token)
    for doc in range(lengths_ref.shape[0] - 1):
        begin = begin + lengths_ref[doc]
        start = jnp.where(token >= begin, begin, start)
    return start


def rotary_tables(lengths_ref, freq_ref, rows, first):
    token = first + lax.broadcasted_iota(jnp.int32, (rows, HEAD_DIM), 0)
    start = doc_starts(lengths_ref, token)
    position = token - start
    angle = position.astype(jnp.float32) * freq_ref[...]
    lane = lax.broadcasted_iota(jnp.int32, (rows, HEAD_DIM), 1)
    sine = jnp.sin(angle)
    return jnp.cos(angle), jnp.where(lane < HALF, -sine, sine), start


def turn(block, cosine, sine):
    x = block.astype(jnp.float32)
    return (x * cosine + pltpu.roll(x, HALF, 1) * sine).astype(jnp.bfloat16)


def pack(out_ref, key_ref, value_ref, cosine, sine):
    for group in range(key_ref.shape[1] // HEAD_DIM):
        cols = slice(group * HEAD_DIM, (group + 1) * HEAD_DIM)
        place = 2 * group * HEAD_DIM
        out_ref[:, place : place + HEAD_DIM] = turn(key_ref[:, cols], cosine, sine)
        out_ref[:, place + HEAD_DIM : place + 2 * HEAD_DIM] = value_ref[:, cols]


def queries_kernel(pieces, lengths_hbm, freq_hbm, key_hbm, value_hbm, query_hbm, *refs):
    pack_ref, start_ref, table_ref = refs[:3]
    turn_refs = refs[3:-6]
    lengths_ref, freq_ref, key_ref, value_ref, query_ref, sems = refs[-6:]
    copies = [
        pltpu.make_async_copy(key_hbm, key_ref, sems.at[0]),
        pltpu.make_async_copy(value_hbm, value_ref, sems.at[1]),
        pltpu.make_async_copy(query_hbm, query_ref, sems.at[2]),
        pltpu.make_async_copy(lengths_hbm, lengths_ref, sems.at[3]),
        pltpu.make_async_copy(freq_hbm, freq_ref, sems.at[4]),
    ]
    for c in copies[::-1]:
        c.start()
    for c in copies[3:]:
        c.wait()
    rows = query_ref.shape[0]
    shard = lax.axis_index("tok")
    cosine, sine, start = rotary_tables(lengths_ref, freq_ref, rows, shard * rows)
    start_ref[...] = start
    for c in copies[:2]:
        c.wait()
    pack(pack_ref, key_ref, value_ref, cosine, sine)
    for p in range(1, pieces + 1):
        far_cosine, far_sine, _ = rotary_tables(lengths_ref, freq_ref, rows, (shard - 2 * p) * rows)
        table_ref[2 * p - 2] = far_cosine
        table_ref[2 * p - 1] = far_sine
    copies[2].wait()
    tiles, stacked, _ = turn_refs[0].shape
    tile = rows // tiles
    per_group = stacked // tile
    for group, out_ref in enumerate(turn_refs):
        for head in range(per_group):
            cols = pl.ds((group * per_group + head) * HEAD_DIM, HEAD_DIM)
            turned = turn(query_ref[:, cols], cosine, sine)
            for t in range(tiles):
                out_ref[t, head * tile : (head + 1) * tile, :] = turned[t * tile : (t + 1) * tile]


def pack_kernel(pieces, table_ref, own_ref, *refs):
    mine_ref, give_ref = refs[-2:]
    relayed = refs[2 * pieces : -2]
    shard = lax.axis_index("tok")
    mine_ref[0] = own_ref[...]
    for p in range(pieces):
        keys = refs[p][...]
        if relayed and not p:
            keys = jnp.where(shard // 2 == 2, relayed[0][...], keys)
        pack(
            mine_ref.at[p + 1],
            keys,
            refs[pieces + p][...],
            table_ref[2 * p],
            table_ref[2 * p + 1],
        )
    odd = lax.rem(shard, 2)
    for p in range(pieces):
        give_ref[p] = mine_ref[p + odd]


def attend_kernel(pieces, per_group, groups, tiles_of, begun, last, *refs):
    norm_ref = None
    if last:
        plan_hbm, refs = refs[0], refs[1:]
        plan_ref, plan_sem = refs[-2:]
        refs = refs[:-2]
        plan_copy = pltpu.make_async_copy(plan_hbm, plan_ref, plan_sem.at[0])
        plan_copy.start()
    start_ref, refs = refs[0], refs[1:]
    if begun:
        norm_ref, refs = refs[0], refs[1:]
    slots = 2 * pieces + 1
    tasks = len(tiles_of)
    mine_ref, theirs_ref = refs[:2]
    refs = refs[2:]
    query_refs, refs = dict(zip(groups, refs)), refs[len(groups) :]
    out_refs, lse_ref = refs[:tasks], refs[tasks]
    staged, norms = refs[tasks + 1 :]
    shard, z = lax.axis_index("tok"), lax.axis_index("kv")
    tiles, stacked, _ = query_refs[groups[0]].shape
    tile = stacked // per_group
    rows = tile * tiles
    def window(group, slot, part):
        place = (2 * group + part) * HEAD_DIM
        cols = slice(place, place + HEAD_DIM)
        back = slots - 1 - slot
        if back % 2 == 0:
            return mine_ref[back // 2, :, cols]
        return theirs_ref[back // 2, :, cols]

    first = shard * rows
    window_first = (shard - (slots - 1)) * rows
    exponent = SCALE * LOG2E
    column = lax.broadcasted_iota(jnp.int32, (tile, HEAD_DIM), 1)
    line = lax.broadcasted_iota(jnp.int32, (tile, HEAD_DIM), 0)
    chunk = min(stacked, 256)
    inside = chunk // tile
    ones = jnp.ones((rows, HEAD_DIM), jnp.bfloat16)
    norms[...] = norm_ref[...] if begun else jnp.zeros(norms.shape, jnp.float32)

    def masks_of(t):
        start = start_ref[pl.ds(pl.multiple_of(t * tile, tile), tile), :]
        masks = []
        for slot in range(slots):
            begins = start - (window_first + slot * rows)
            for lane in range(0, rows, HEAD_DIM):
                allowed = column + lane >= begins
                if slot == slots - 1:
                    allowed = allowed & (column + lane <= line + t * tile)
                masks.append(allowed[None])
        return masks

    def scores_of(group, t, c, masks):
        q = query_refs[group][t, c * chunk : (c + 1) * chunk, :]
        parts, best = [], None
        for slot in range(slots):
            block = lax.dot_general(
                q,
                window(group, slot, 0),
                (((1,), (1,)), ((), ())),
                preferred_element_type=jnp.float32,
            )
            for lane in range(0, rows, HEAD_DIM):
                part = block[:, lane : lane + HEAD_DIM].reshape(inside, tile, HEAD_DIM)
                part = jnp.where(masks[len(parts)], part, NEG).reshape(chunk, HEAD_DIM)
                parts.append(part)
                best = part if best is None else jnp.maximum(best, part)
        return parts, best

    def mix(index, c, i, parts, best, gathered):
        group = groups[index]
        top = jnp.max(best, axis=1, keepdims=True) * exponent
        mixed = None
        per_slot = rows // HEAD_DIM
        for slot in range(slots):
            probs = []
            for part in parts[per_slot * slot : per_slot * (slot + 1)]:
                weights = jnp.exp2(part * exponent - top)
                probs.append(weights.astype(jnp.bfloat16))
            values = jnp.concatenate([window(group, slot, 1), ones], axis=1)
            product = jnp.dot(
                jnp.concatenate(probs, axis=1), values, preferred_element_type=jnp.float32
            )
            mixed = product if mixed is None else mixed + product
        row_sum = mixed[:, HEAD_DIM:]
        result = (mixed[:, :HEAD_DIM] / row_sum).astype(jnp.bfloat16)
        norm = top * (1.0 / LOG2E) + jnp.log(row_sum)
        for h in range(inside):
            head = c * inside + h
            part = slice(h * tile, (h + 1) * tile)
            column_of = (index * per_group + head) * HEAD_DIM
            staged[i, :, column_of : column_of + HEAD_DIM] = result[part]
            gathered = jnp.where(column == group * per_group + head, norm[part], gathered)
        return gathered

    def step(i, carry):
        t = lax.rem(z + tiles_of.start + i * tiles_of.step, tiles)
        here = pl.ds(pl.multiple_of(t * tile, tile), tile)
        gathered = norms[here, :]
        masks = masks_of(t)
        jobs = [(index, c) for index in range(len(groups)) for c in range(stacked // chunk)]
        ready = scores_of(groups[0], t, 0, masks)
        for job, (index, c) in enumerate(jobs):
            following = None
            if job + 1 < len(jobs):
                next_index, next_c = jobs[job + 1]
                following = scores_of(groups[next_index], t, next_c, masks)
            gathered = mix(index, c, i, *ready, gathered)
            ready = following
        norms[here, :] = gathered
        return carry

    lax.fori_loop(0, len(tiles_of), step, 0, unroll=slots <= 5)

    for position, out_ref in enumerate(out_refs):
        out_ref[...] = staged[position]
    if last:
        plan_copy.wait()
        shards = plan_ref.shape[0]
        block = rows // shards
        for s in range(shards):
            picked = pl.multiple_of(plan_ref[shard, s] * block, block)
            lse_ref[s * block : (s + 1) * block, :] = norms[pl.ds(picked, block), :]
    else:
        lse_ref[...] = norms[...]


def placed(planes, width, groups, places, pieces, out_ref, sems):
    z = lax.axis_index("kv")
    copies = []
    for index, (s, group) in enumerate(places):
        origin = lax.rem(z - s + planes, planes)
        column = pl.multiple_of((origin * groups + group) * width, width)
        target = out_ref.at[:, pl.ds(column, pieces[index].shape[1])]
        copies.append(pltpu.make_async_copy(pieces[index], target, sems.at[index]))
    return copies


def begin_kernel(planes, width, groups, places, *refs):
    pieces, out_ref, sems = refs[:-2], *refs[-2:]
    copies = placed(planes, width, groups, places, pieces, out_ref, sems)
    for c in copies:
        c.start()
    for c in copies:
        c.wait()


def assemble_kernel(planes, width, groups, places, served_ref, *refs):
    pieces, out_ref, lse_hbm, lse_ref, sems = refs[:-5], *refs[-4:]
    copies = placed(planes, width, groups, places, pieces, out_ref, sems)
    for c in copies:
        c.start()
    lse_ref[...] = served_ref[...].T[: lse_ref.shape[0]]
    lse_copy = pltpu.make_async_copy(lse_ref, lse_hbm, sems.at[len(pieces)])
    lse_copy.start()
    for c in copies:
        c.wait()
    lse_copy.wait()


def body(queries, key_states, value_states, doc_lengths, block_plan):
    shards = lax.axis_size("tok")
    planes = lax.axis_size("kv")
    rows = queries.shape[0]
    groups = key_states.shape[1] // HEAD_DIM
    heads = queries.shape[1] // HEAD_DIM
    per_group = heads // groups
    tile = rows // planes
    pieces = shards // 4
    half_freq = THETA ** (-np.arange(HALF, dtype=np.float64) * 2.0 / HEAD_DIM)
    freq = jnp.asarray(np.concatenate([half_freq, half_freq])[None, :], jnp.float32)

    pair = [(i, i ^ 1) for i in range(shards)]

    def forward(x, p):
        return lax.ppermute(x, "tok", [(i, i + 2 * p) for i in range(shards - 2 * p)])

    far_keys = [forward(key_states, p) for p in range(1, pieces + 1)]
    far_values = [forward(value_states, p) for p in range(1, pieces + 1)]
    relayed = []
    after = queries
    if shards == 8:
        far_keys[0] = lax.ppermute(key_states, "tok", [(0, 2), (1, 3), (4, 6), (5, 7)])
        relayed = [lax.ppermute(far_keys[1], "tok", [(6, 4), (7, 5)])]
        after, _ = lax.optimization_barrier((queries, far_keys[1]))
    pack_shape = jax.ShapeDtypeStruct((rows, 2 * groups * HEAD_DIM), jnp.bfloat16)
    with jax.named_scope("rotate"):
        result = pl.pallas_call(
            partial(queries_kernel, pieces),
            out_shape=[
                pack_shape,
                jax.ShapeDtypeStruct((rows, HEAD_DIM), jnp.int32),
                jax.ShapeDtypeStruct((2 * pieces, rows, HEAD_DIM), jnp.float32),
            ]
            + [jax.ShapeDtypeStruct((planes, per_group * tile, HEAD_DIM), jnp.bfloat16)] * groups,
            in_specs=[hbm()] * 5,
            out_specs=[vmem()] * (3 + groups),
            scratch_shapes=[
                pltpu.SMEM(doc_lengths.shape, jnp.int32),
                pltpu.VMEM(freq.shape, jnp.float32),
                pltpu.VMEM(key_states.shape, jnp.bfloat16),
                pltpu.VMEM(value_states.shape, jnp.bfloat16),
                pltpu.VMEM(queries.shape, jnp.bfloat16),
                pltpu.SemaphoreType.DMA((5,)),
            ],
            compiler_params=params(),
            cost_estimate=cost(3.0),
        )(
            pltpu.with_memory_space_constraint(doc_lengths, pltpu.HBM),
            pltpu.with_memory_space_constraint(freq, pltpu.HBM),
            pltpu.with_memory_space_constraint(key_states, pltpu.HBM),
            pltpu.with_memory_space_constraint(value_states, pltpu.HBM),
            pltpu.with_memory_space_constraint(after, pltpu.HBM),
        )
    own, start, tables = result[:3]
    turned = result[3:]
    with jax.named_scope("pack"):
        mine, give = pl.pallas_call(
            partial(pack_kernel, pieces),
            out_shape=[
                jax.ShapeDtypeStruct((count, *pack_shape.shape), jnp.bfloat16)
                for count in (pieces + 1, pieces)
            ],
            in_specs=[vmem()] * (2 + 2 * pieces + len(relayed)),
            out_specs=[vmem()] * 2,
            compiler_params=params(),
            cost_estimate=cost(1.0),
        )(tables, own, *far_keys, *far_values, *relayed)
    theirs = lax.ppermute(give, "tok", pair)

    def attend(norm, used, tiles_of, last, microseconds):
        plan = [pltpu.with_memory_space_constraint(block_plan, pltpu.HBM)] if last else []
        operands = [start] if norm is None else [start, norm]
        operands += [mine, theirs] + [turned[group] for group in used]
        tasks = len(tiles_of)
        width = len(used) * per_group * HEAD_DIM
        with jax.named_scope("attend"):
            result = pl.pallas_call(
                partial(
                    attend_kernel, pieces, per_group, used, tiles_of, norm is not None, last
                ),
                out_shape=[jax.ShapeDtypeStruct((tile, width), jnp.bfloat16)]
                * tasks
                + [jax.ShapeDtypeStruct((rows, HEAD_DIM), jnp.float32)],
                in_specs=[hbm()] * len(plan) + [vmem()] * len(operands),
                out_specs=[vmem()] * (tasks + 1),
                scratch_shapes=[
                    pltpu.VMEM((tasks, tile, width), jnp.bfloat16),
                    pltpu.VMEM((rows, HEAD_DIM), jnp.float32),
                ]
                + [pltpu.SMEM(block_plan.shape, jnp.int32), pltpu.SemaphoreType.DMA((1,))]
                * len(plan),
                compiler_params=params(),
                cost_estimate=cost(microseconds),
            )(*plan, *operands)
        return result[:tasks], result[tasks]

    def send(piece, s):
        return lax.ppermute(piece, "kv", [(i, (i + s) % planes) for i in range(planes)])

    norm, pieces_of = None, {}
    both = list(range(groups))
    for span in (range(1, 2), range(2, planes)):
        result, norm = attend(norm, both, span, False, 4.0 * len(span))
        for s, piece in zip(span, result):
            pieces_of[s, 0] = send(piece, s)
    (piece,), norm = attend(norm, both, range(1), True, 4.0)
    pieces_of[0, 0] = piece
    block_rows = rows // shards
    served = lax.all_to_all(
        norm.reshape(shards, block_rows, HEAD_DIM), "tok", split_axis=0, concat_axis=0, tiled=True
    ).reshape(rows, HEAD_DIM)
    width = per_group * HEAD_DIM
    out_shape = jax.ShapeDtypeStruct((tile, planes * heads * HEAD_DIM), jnp.bfloat16)
    soon = [place for place in sorted(pieces_of) if place[0] < 2]
    late = [place for place in sorted(pieces_of) if place[0] >= 2]
    with jax.named_scope("begin"):
        begun = pl.pallas_call(
            partial(begin_kernel, planes, width, groups, soon),
            out_shape=out_shape,
            in_specs=[hbm()] * len(soon),
            out_specs=hbm(),
            scratch_shapes=[pltpu.SemaphoreType.DMA((len(soon),))],
            compiler_params=params(),
        )(*[pieces_of[place] for place in soon])
    with jax.named_scope("assemble"):
        attention_out, served_lse = pl.pallas_call(
            partial(assemble_kernel, planes, width, groups, late),
            out_shape=[out_shape, jax.ShapeDtypeStruct((heads, rows), jnp.float32)],
            in_specs=[vmem()] + [hbm()] * (len(late) + 1),
            out_specs=[hbm(), hbm()],
            scratch_shapes=[
                pltpu.VMEM((heads, rows), jnp.float32),
                pltpu.SemaphoreType.DMA((len(late) + 1,)),
            ],
            input_output_aliases={len(late) + 1: 0},
            compiler_params=params(),
        )(served, *[pieces_of[place] for place in late], begun)
    return (attention_out, served_lse)


def solution(mesh):
    return jax.shard_map(
        body,
        mesh=mesh,
        in_specs=(P("tok", "kv"), P("tok", "kv"), P("tok", "kv"), P(), P()),
        out_specs=(P(("tok", "kv"), None), P("kv", "tok")),
        check_vma=False,
    )
```

```python
import math
from functools import partial

import jax
import jax.numpy as jnp
import numpy as np
from jax import lax
from jax.experimental import pallas as pl
from jax.experimental.pallas import tpu as pltpu
from jax.sharding import PartitionSpec as P

HEAD_DIM = 128
HALF = HEAD_DIM // 2
THETA = 500000.0
NEG = -1e30
LOG2E = math.log2(math.e)
SCALE = 1.0 / math.sqrt(HEAD_DIM)
VMEM_LIMIT = 48 * 1024 * 1024


def vmem():
    return pl.BlockSpec(memory_space=pltpu.VMEM)


def smem():
    return pl.BlockSpec(memory_space=pltpu.SMEM)


def hbm():
    return pl.BlockSpec(memory_space=pl.ANY)


def far_hbm():
    return pl.BlockSpec(memory_space=pltpu.HBM)


def params():
    return pltpu.CompilerParams(vmem_limit_bytes=VMEM_LIMIT)


def cost(microseconds):
    return pl.CostEstimate(flops=int(microseconds * 1.15e9), bytes_accessed=0, transcendentals=0)


def doc_starts(lengths_ref, token):
    begin = jnp.int32(0)
    start = jnp.zeros_like(token)
    for doc in range(lengths_ref.shape[0] - 1):
        begin = begin + lengths_ref[doc]
        start = jnp.where(token >= begin, begin, start)
    return start


def rotary_tables(lengths_ref, freq_ref, rows, first):
    token = first + lax.broadcasted_iota(jnp.int32, (rows, HEAD_DIM), 0)
    start = doc_starts(lengths_ref, token)
    position = token - start
    angle = position.astype(jnp.float32) * freq_ref[...]
    lane = lax.broadcasted_iota(jnp.int32, (rows, HEAD_DIM), 1)
    sine = jnp.sin(angle)
    return jnp.cos(angle), jnp.where(lane < HALF, -sine, sine), start


def turn(block, cosine, sine):
    x = block.astype(jnp.float32)
    return (x * cosine + pltpu.roll(x, HALF, 1) * sine).astype(jnp.bfloat16)


def pack(out_ref, key_ref, value_ref, cosine, sine):
    for group in range(key_ref.shape[1] // HEAD_DIM):
        cols = slice(group * HEAD_DIM, (group + 1) * HEAD_DIM)
        place = 2 * group * HEAD_DIM
        out_ref[:, place : place + HEAD_DIM] = turn(key_ref[:, cols], cosine, sine)
        out_ref[:, place + HEAD_DIM : place + 2 * HEAD_DIM] = value_ref[:, cols]


def queries_kernel(pieces, lengths_hbm, freq_hbm, key_hbm, value_hbm, query_hbm, *refs):
    pack_ref, start_ref, table_ref = refs[:3]
    turn_refs = refs[3:-6]
    lengths_ref, freq_ref, key_ref, value_ref, query_ref, sems = refs[-6:]
    copies = [
        pltpu.make_async_copy(key_hbm, key_ref, sems.at[0]),
        pltpu.make_async_copy(value_hbm, value_ref, sems.at[1]),
        pltpu.make_async_copy(query_hbm, query_ref, sems.at[2]),
        pltpu.make_async_copy(lengths_hbm, lengths_ref, sems.at[3]),
        pltpu.make_async_copy(freq_hbm, freq_ref, sems.at[4]),
    ]
    for c in copies[::-1]:
        c.start()
    for c in copies[3:]:
        c.wait()
    rows = query_ref.shape[0]
    shard = lax.axis_index("tok")
    cosine, sine, start = rotary_tables(lengths_ref, freq_ref, rows, shard * rows)
    start_ref[...] = start
    for c in copies[:2]:
        c.wait()
    pack(pack_ref, key_ref, value_ref, cosine, sine)
    for p in range(1, pieces + 1):
        far_cosine, far_sine, _ = rotary_tables(lengths_ref, freq_ref, rows, (shard - 2 * p) * rows)
        table_ref[2 * p - 2] = far_cosine
        table_ref[2 * p - 1] = far_sine
    copies[2].wait()
    tiles, stacked, _ = turn_refs[0].shape
    tile = rows // tiles
    per_group = stacked // tile
    for group, out_ref in enumerate(turn_refs):
        for head in range(per_group):
            cols = pl.ds((group * per_group + head) * HEAD_DIM, HEAD_DIM)
            turned = turn(query_ref[:, cols], cosine, sine)
            for t in range(tiles):
                out_ref[t, head * tile : (head + 1) * tile, :] = turned[t * tile : (t + 1) * tile]


def pack_kernel(pieces, table_ref, own_ref, *refs):
    mine_ref, give_ref = refs[-2:]
    relayed = refs[2 * pieces : -2]
    shard = lax.axis_index("tok")
    mine_ref[0] = own_ref[...]
    for p in range(pieces):
        keys = refs[p][...]
        if relayed and not p:
            keys = jnp.where(shard // 2 == 2, relayed[0][...], keys)
        pack(
            mine_ref.at[p + 1],
            keys,
            refs[pieces + p][...],
            table_ref[2 * p],
            table_ref[2 * p + 1],
        )
    odd = lax.rem(shard, 2)
    for p in range(pieces):
        give_ref[p] = mine_ref[p + odd]


def attend_kernel(pieces, per_group, groups, tiles_of, begun, last, *refs):
    norm_ref = None
    if last:
        plan_hbm, refs = refs[0], refs[1:]
        plan_ref, plan_sem = refs[-2:]
        refs = refs[:-2]
        plan_copy = pltpu.make_async_copy(plan_hbm, plan_ref, plan_sem.at[0])
        plan_copy.start()
    start_ref, refs = refs[0], refs[1:]
    if begun:
        norm_ref, refs = refs[0], refs[1:]
    slots = 2 * pieces + 1
    tasks = len(tiles_of)
    mine_ref, theirs_ref = refs[:2]
    refs = refs[2:]
    query_refs, refs = dict(zip(groups, refs)), refs[len(groups) :]
    out_refs, lse_ref = refs[:tasks], refs[tasks]
    staged, norms = refs[tasks + 1 :]
    shard, z = lax.axis_index("tok"), lax.axis_index("kv")
    tiles, stacked, _ = query_refs[groups[0]].shape
    tile = stacked // per_group
    rows = tile * tiles
    def window(group, slot, part):
        place = (2 * group + part) * HEAD_DIM
        cols = slice(place, place + HEAD_DIM)
        back = slots - 1 - slot
        if back % 2 == 0:
            return mine_ref[back // 2, :, cols]
        return theirs_ref[back // 2, :, cols]

    first = shard * rows
    window_first = (shard - (slots - 1)) * rows
    exponent = SCALE * LOG2E
    column = lax.broadcasted_iota(jnp.int32, (tile, HEAD_DIM), 1)
    line = lax.broadcasted_iota(jnp.int32, (tile, HEAD_DIM), 0)
    chunk = min(stacked, 256)
    inside = chunk // tile
    ones = jnp.ones((rows, HEAD_DIM), jnp.bfloat16)
    unrolled = slots <= 5
    norms[...] = norm_ref[...] if begun else jnp.zeros(norms.shape, jnp.float32)

    def masks_of(t):
        start = start_ref[pl.ds(pl.multiple_of(t * tile, tile), tile), :]
        masks = []
        for slot in range(slots):
            begins = start - (window_first + slot * rows)
            for lane in range(0, rows, HEAD_DIM):
                allowed = column + lane >= begins
                if slot == slots - 1:
                    allowed = allowed & (column + lane <= line + t * tile)
                masks.append(allowed[None])
        return masks

    def scores_of(group, t, c, masks):
        q = query_refs[group][t, c * chunk : (c + 1) * chunk, :]
        parts, best = [], None
        for slot in range(slots):
            block = lax.dot_general(
                q,
                window(group, slot, 0),
                (((1,), (1,)), ((), ())),
                preferred_element_type=jnp.float32,
            )
            for lane in range(0, rows, HEAD_DIM):
                part = block[:, lane : lane + HEAD_DIM].reshape(inside, tile, HEAD_DIM)
                part = jnp.where(masks[len(parts)], part, NEG).reshape(chunk, HEAD_DIM)
                parts.append(part)
                best = part if best is None else jnp.maximum(best, part)
        return parts, best

    def mix(index, c, i, parts, best, gathered):
        group = groups[index]
        top = jnp.max(best, axis=1, keepdims=True) * exponent
        mixed = None
        per_slot = rows // HEAD_DIM
        for slot in range(slots):
            probs = []
            for part in parts[per_slot * slot : per_slot * (slot + 1)]:
                weights = jnp.exp2(part * exponent - top)
                probs.append(weights.astype(jnp.bfloat16))
            values = jnp.concatenate([window(group, slot, 1), ones], axis=1)
            product = jnp.dot(
                jnp.concatenate(probs, axis=1), values, preferred_element_type=jnp.float32
            )
            mixed = product if mixed is None else mixed + product
        row_sum = mixed[:, HEAD_DIM:]
        result = (mixed[:, :HEAD_DIM] / row_sum).astype(jnp.bfloat16)
        norm = top * (1.0 / LOG2E) + jnp.log(row_sum)
        for h in range(inside):
            head = c * inside + h
            part = slice(h * tile, (h + 1) * tile)
            column_of = (index * per_group + head) * HEAD_DIM
            if unrolled:
                out_refs[i][:, column_of : column_of + HEAD_DIM] = result[part]
            else:
                staged[i, :, column_of : column_of + HEAD_DIM] = result[part]
            gathered = jnp.where(column == group * per_group + head, norm[part], gathered)
        return gathered

    def step(i, carry):
        t = lax.rem(z + tiles_of.start + i * tiles_of.step, tiles)
        here = pl.ds(pl.multiple_of(t * tile, tile), tile)
        gathered = norms[here, :]
        masks = masks_of(t)
        jobs = [(index, c) for index in range(len(groups)) for c in range(stacked // chunk)]
        ready = scores_of(groups[0], t, 0, masks)
        for job, (index, c) in enumerate(jobs):
            following = None
            if job + 1 < len(jobs):
                next_index, next_c = jobs[job + 1]
                following = scores_of(groups[next_index], t, next_c, masks)
            gathered = mix(index, c, i, *ready, gathered)
            ready = following
        norms[here, :] = gathered
        return carry

    if unrolled:
        for i in range(len(tiles_of)):
            step(i, 0)
    else:
        lax.fori_loop(0, len(tiles_of), step, 0)
        for position, out_ref in enumerate(out_refs):
            out_ref[...] = staged[position]
    if last:
        plan_copy.wait()
        shards = plan_ref.shape[0]
        block = rows // shards
        for s in range(shards):
            picked = pl.multiple_of(plan_ref[shard, s] * block, block)
            lse_ref[s * block : (s + 1) * block, :] = norms[pl.ds(picked, block), :]
    else:
        lse_ref[...] = norms[...]


def placed(planes, width, groups, places, pieces, out_ref, sems):
    z = lax.axis_index("kv")
    copies = []
    for index, (s, group) in enumerate(places):
        origin = lax.rem(z - s + planes, planes)
        column = pl.multiple_of((origin * groups + group) * width, width)
        target = out_ref.at[:, pl.ds(column, pieces[index].shape[1])]
        copies.append(pltpu.make_async_copy(pieces[index], target, sems.at[index]))
    return copies


def begin_kernel(planes, width, groups, places, *refs):
    pieces, out_ref, sems = refs[:-2], *refs[-2:]
    copies = placed(planes, width, groups, places, pieces, out_ref, sems)
    for c in copies:
        c.start()
    for c in copies:
        c.wait()


def assemble_kernel(planes, width, groups, places, served_ref, *refs):
    pieces, out_ref, lse_hbm, lse_ref, sems = refs[:-5], *refs[-4:]
    copies = placed(planes, width, groups, places, pieces, out_ref, sems)
    for c in copies:
        c.start()
    lse_ref[...] = served_ref[...].T[: lse_ref.shape[0]]
    lse_copy = pltpu.make_async_copy(lse_ref, lse_hbm, sems.at[len(pieces)])
    lse_copy.start()
    for c in copies:
        c.wait()
    lse_copy.wait()


def body(queries, key_states, value_states, doc_lengths, block_plan):
    shards = lax.axis_size("tok")
    planes = lax.axis_size("kv")
    rows = queries.shape[0]
    groups = key_states.shape[1] // HEAD_DIM
    heads = queries.shape[1] // HEAD_DIM
    per_group = heads // groups
    tile = rows // planes
    pieces = shards // 4
    half_freq = THETA ** (-np.arange(HALF, dtype=np.float64) * 2.0 / HEAD_DIM)
    freq = jnp.asarray(np.concatenate([half_freq, half_freq])[None, :], jnp.float32)

    pair = [(i, i ^ 1) for i in range(shards)]

    def forward(x, p):
        return lax.ppermute(x, "tok", [(i, i + 2 * p) for i in range(shards - 2 * p)])

    far_keys = [forward(key_states, p) for p in range(1, pieces + 1)]
    far_values = [forward(value_states, p) for p in range(1, pieces + 1)]
    relayed = []
    after = queries
    if shards == 8:
        far_keys[0] = lax.ppermute(key_states, "tok", [(0, 2), (1, 3), (4, 6), (5, 7)])
        relayed = [lax.ppermute(far_keys[1], "tok", [(6, 4), (7, 5)])]
        after, _ = lax.optimization_barrier((queries, far_keys[1]))
    pack_shape = jax.ShapeDtypeStruct((rows, 2 * groups * HEAD_DIM), jnp.bfloat16)
    with jax.named_scope("rotate"):
        result = pl.pallas_call(
            partial(queries_kernel, pieces),
            out_shape=[
                pack_shape,
                jax.ShapeDtypeStruct((rows, HEAD_DIM), jnp.int32),
                jax.ShapeDtypeStruct((2 * pieces, rows, HEAD_DIM), jnp.float32),
            ]
            + [jax.ShapeDtypeStruct((planes, per_group * tile, HEAD_DIM), jnp.bfloat16)] * groups,
            in_specs=[hbm()] * 5,
            out_specs=[vmem()] * (3 + groups),
            scratch_shapes=[
                pltpu.SMEM(doc_lengths.shape, jnp.int32),
                pltpu.VMEM(freq.shape, jnp.float32),
                pltpu.VMEM(key_states.shape, jnp.bfloat16),
                pltpu.VMEM(value_states.shape, jnp.bfloat16),
                pltpu.VMEM(queries.shape, jnp.bfloat16),
                pltpu.SemaphoreType.DMA((5,)),
            ],
            compiler_params=params(),
            cost_estimate=cost(3.0),
        )(
            pltpu.with_memory_space_constraint(doc_lengths, pltpu.HBM),
            pltpu.with_memory_space_constraint(freq, pltpu.HBM),
            pltpu.with_memory_space_constraint(key_states, pltpu.HBM),
            pltpu.with_memory_space_constraint(value_states, pltpu.HBM),
            pltpu.with_memory_space_constraint(after, pltpu.HBM),
        )
    own, start, tables = result[:3]
    turned = result[3:]
    with jax.named_scope("pack"):
        mine, give = pl.pallas_call(
            partial(pack_kernel, pieces),
            out_shape=[
                jax.ShapeDtypeStruct((count, *pack_shape.shape), jnp.bfloat16)
                for count in (pieces + 1, pieces)
            ],
            in_specs=[vmem()] * (2 + 2 * pieces + len(relayed)),
            out_specs=[vmem()] * 2,
            compiler_params=params(),
            cost_estimate=cost(1.0),
        )(tables, own, *far_keys, *far_values, *relayed)
    theirs = lax.ppermute(give, "tok", pair)

    def attend(norm, used, tiles_of, last, microseconds):
        plan = [pltpu.with_memory_space_constraint(block_plan, pltpu.HBM)] if last else []
        operands = [start] if norm is None else [start, norm]
        operands += [mine, theirs] + [turned[group] for group in used]
        tasks = len(tiles_of)
        width = len(used) * per_group * HEAD_DIM
        with jax.named_scope("attend"):
            result = pl.pallas_call(
                partial(
                    attend_kernel, pieces, per_group, used, tiles_of, norm is not None, last
                ),
                out_shape=[jax.ShapeDtypeStruct((tile, width), jnp.bfloat16)]
                * tasks
                + [jax.ShapeDtypeStruct((rows, HEAD_DIM), jnp.float32)],
                in_specs=[hbm()] * len(plan) + [vmem()] * len(operands),
                out_specs=[vmem()] * (tasks + 1),
                scratch_shapes=[
                    pltpu.VMEM((tasks, tile, width), jnp.bfloat16),
                    pltpu.VMEM((rows, HEAD_DIM), jnp.float32),
                ]
                + [pltpu.SMEM(block_plan.shape, jnp.int32), pltpu.SemaphoreType.DMA((1,))]
                * len(plan),
                compiler_params=params(),
                cost_estimate=cost(microseconds),
            )(*plan, *operands)
        return result[:tasks], result[tasks]

    def send(piece, s):
        return lax.ppermute(piece, "kv", [(i, (i + s) % planes) for i in range(planes)])

    norm, pieces_of = None, {}
    both = list(range(groups))
    for span in (range(1, 2), range(2, planes)):
        result, norm = attend(norm, both, span, False, 4.0 * len(span))
        for s, piece in zip(span, result):
            pieces_of[s, 0] = send(piece, s)
    (piece,), norm = attend(norm, both, range(1), True, 4.0)
    pieces_of[0, 0] = piece
    block_rows = rows // shards
    served = lax.all_to_all(
        norm.reshape(shards, block_rows, HEAD_DIM), "tok", split_axis=0, concat_axis=0, tiled=True
    ).reshape(rows, HEAD_DIM)
    width = per_group * HEAD_DIM
    out_shape = jax.ShapeDtypeStruct((tile, planes * heads * HEAD_DIM), jnp.bfloat16)
    soon = [place for place in sorted(pieces_of) if place[0] < 2]
    late = [place for place in sorted(pieces_of) if place[0] >= 2]
    with jax.named_scope("begin"):
        begun = pl.pallas_call(
            partial(begin_kernel, planes, width, groups, soon),
            out_shape=out_shape,
            in_specs=[hbm()] * len(soon),
            out_specs=hbm(),
            scratch_shapes=[pltpu.SemaphoreType.DMA((len(soon),))],
            compiler_params=params(),
        )(*[pieces_of[place] for place in soon])
    with jax.named_scope("assemble"):
        attention_out, served_lse = pl.pallas_call(
            partial(assemble_kernel, planes, width, groups, late),
            out_shape=[out_shape, jax.ShapeDtypeStruct((heads, rows), jnp.float32)],
            in_specs=[vmem()] + [hbm()] * (len(late) + 1),
            out_specs=[hbm(), hbm()],
            scratch_shapes=[
                pltpu.VMEM((heads, rows), jnp.float32),
                pltpu.SemaphoreType.DMA((len(late) + 1,)),
            ],
            input_output_aliases={len(late) + 1: 0},
            compiler_params=params(),
        )(served, *[pieces_of[place] for place in late], begun)
    return (attention_out, served_lse)


def solution(mesh):
    return jax.shard_map(
        body,
        mesh=mesh,
        in_specs=(P("tok", "kv"), P("tok", "kv"), P("tok", "kv"), P(), P()),
        out_specs=(P(("tok", "kv"), None), P("kv", "tok")),
        check_vma=False,
    )
```

```python
import math
from functools import partial

import jax
import jax.numpy as jnp
import numpy as np
from jax import lax
from jax.experimental import pallas as pl
from jax.experimental.pallas import tpu as pltpu
from jax.sharding import PartitionSpec as P

HEAD_DIM = 128
HALF = HEAD_DIM // 2
THETA = 500000.0
NEG = -1e30
LOG2E = math.log2(math.e)
SCALE = 1.0 / math.sqrt(HEAD_DIM)
VMEM_LIMIT = 48 * 1024 * 1024


def vmem():
    return pl.BlockSpec(memory_space=pltpu.VMEM)


def smem():
    return pl.BlockSpec(memory_space=pltpu.SMEM)


def hbm():
    return pl.BlockSpec(memory_space=pl.ANY)


def far_hbm():
    return pl.BlockSpec(memory_space=pltpu.HBM)


def params():
    return pltpu.CompilerParams(vmem_limit_bytes=VMEM_LIMIT)


def cost(microseconds):
    return pl.CostEstimate(flops=int(microseconds * 1.15e9), bytes_accessed=0, transcendentals=0)


def doc_starts(lengths_ref, token):
    begin = jnp.int32(0)
    start = jnp.zeros_like(token)
    for doc in range(lengths_ref.shape[0] - 1):
        begin = begin + lengths_ref[doc]
        start = jnp.where(token >= begin, begin, start)
    return start


def rotary_tables(lengths_ref, freq_ref, rows, first):
    token = first + lax.broadcasted_iota(jnp.int32, (rows, HEAD_DIM), 0)
    start = doc_starts(lengths_ref, token)
    position = token - start
    angle = position.astype(jnp.float32) * freq_ref[...]
    lane = lax.broadcasted_iota(jnp.int32, (rows, HEAD_DIM), 1)
    sine = jnp.sin(angle)
    return jnp.cos(angle), jnp.where(lane < HALF, -sine, sine), start


def turn(block, cosine, sine):
    x = block.astype(jnp.float32)
    return (x * cosine + pltpu.roll(x, HALF, 1) * sine).astype(jnp.bfloat16)


def pack(out_ref, key_ref, value_ref, cosine, sine):
    for group in range(key_ref.shape[1] // HEAD_DIM):
        cols = slice(group * HEAD_DIM, (group + 1) * HEAD_DIM)
        place = 2 * group * HEAD_DIM
        out_ref[:, place : place + HEAD_DIM] = turn(key_ref[:, cols], cosine, sine)
        out_ref[:, place + HEAD_DIM : place + 2 * HEAD_DIM] = value_ref[:, cols]


def queries_kernel(pieces, lengths_hbm, freq_hbm, key_hbm, value_hbm, query_hbm, *refs):
    pack_ref, start_ref, table_ref = refs[:3]
    turn_refs = refs[3:-6]
    lengths_ref, freq_ref, key_ref, value_ref, query_ref, sems = refs[-6:]
    copies = [
        pltpu.make_async_copy(key_hbm, key_ref, sems.at[0]),
        pltpu.make_async_copy(value_hbm, value_ref, sems.at[1]),
        pltpu.make_async_copy(query_hbm, query_ref, sems.at[2]),
        pltpu.make_async_copy(lengths_hbm, lengths_ref, sems.at[3]),
        pltpu.make_async_copy(freq_hbm, freq_ref, sems.at[4]),
    ]
    for c in copies[::-1]:
        c.start()
    for c in copies[3:]:
        c.wait()
    rows = query_ref.shape[0]
    shard = lax.axis_index("tok")
    cosine, sine, start = rotary_tables(lengths_ref, freq_ref, rows, shard * rows)
    start_ref[...] = start
    for c in copies[:2]:
        c.wait()
    pack(pack_ref, key_ref, value_ref, cosine, sine)
    for p in range(1, pieces + 1):
        far_cosine, far_sine, _ = rotary_tables(lengths_ref, freq_ref, rows, (shard - 2 * p) * rows)
        table_ref[2 * p - 2] = far_cosine
        table_ref[2 * p - 1] = far_sine
    copies[2].wait()
    tiles, stacked, _ = turn_refs[0].shape
    tile = rows // tiles
    per_group = stacked // tile
    for group, out_ref in enumerate(turn_refs):
        for head in range(per_group):
            cols = pl.ds((group * per_group + head) * HEAD_DIM, HEAD_DIM)
            turned = turn(query_ref[:, cols], cosine, sine)
            for t in range(tiles):
                out_ref[t, head * tile : (head + 1) * tile, :] = turned[t * tile : (t + 1) * tile]


def pack_kernel(pieces, table_ref, own_ref, *refs):
    mine_ref, give_ref = refs[-2:]
    relayed = refs[2 * pieces : -2]
    shard = lax.axis_index("tok")
    mine_ref[0] = own_ref[...]
    for p in range(pieces):
        keys = refs[p][...]
        if relayed and not p:
            keys = jnp.where(shard // 2 == 2, relayed[0][...], keys)
        pack(
            mine_ref.at[p + 1],
            keys,
            refs[pieces + p][...],
            table_ref[2 * p],
            table_ref[2 * p + 1],
        )
    odd = lax.rem(shard, 2)
    for p in range(pieces):
        give_ref[p] = mine_ref[p + odd]


def attend_kernel(pieces, per_group, groups, tiles_of, begun, last, *refs):
    norm_ref = None
    if last:
        plan_hbm, refs = refs[0], refs[1:]
        plan_ref, plan_sem = refs[-2:]
        refs = refs[:-2]
        plan_copy = pltpu.make_async_copy(plan_hbm, plan_ref, plan_sem.at[0])
        plan_copy.start()
    start_ref, refs = refs[0], refs[1:]
    if begun:
        norm_ref, refs = refs[0], refs[1:]
    slots = 2 * pieces + 1
    tasks = len(tiles_of)
    mine_ref, theirs_ref = refs[:2]
    refs = refs[2:]
    query_refs, refs = dict(zip(groups, refs)), refs[len(groups) :]
    out_refs, lse_ref = refs[:tasks], refs[tasks]
    staged, norms = refs[tasks + 1 :]
    shard, z = lax.axis_index("tok"), lax.axis_index("kv")
    tiles, stacked, _ = query_refs[groups[0]].shape
    tile = stacked // per_group
    rows = tile * tiles
    def window(group, slot, part):
        place = (2 * group + part) * HEAD_DIM
        cols = slice(place, place + HEAD_DIM)
        back = slots - 1 - slot
        if back % 2 == 0:
            return mine_ref[back // 2, :, cols]
        return theirs_ref[back // 2, :, cols]

    first = shard * rows
    window_first = (shard - (slots - 1)) * rows
    exponent = SCALE * LOG2E
    column = lax.broadcasted_iota(jnp.int32, (tile, HEAD_DIM), 1)
    line = lax.broadcasted_iota(jnp.int32, (tile, HEAD_DIM), 0)
    chunk = min(stacked, 256)
    inside = chunk // tile
    ones = jnp.ones((rows, HEAD_DIM), jnp.bfloat16)
    unrolled = slots <= 5
    norms[...] = norm_ref[...] if begun else jnp.zeros(norms.shape, jnp.float32)

    def masks_of(t):
        start = start_ref[pl.ds(pl.multiple_of(t * tile, tile), tile), :]
        masks = []
        for slot in range(slots):
            begins = start - (window_first + slot * rows)
            for lane in range(0, rows, HEAD_DIM):
                allowed = column + lane >= begins
                if slot == slots - 1:
                    allowed = allowed & (column + lane <= line + t * tile)
                masks.append(allowed[None])
        return masks

    def scores_of(group, t, c, masks):
        q = query_refs[group][t, c * chunk : (c + 1) * chunk, :]
        parts, best = [], None
        for slot in range(slots):
            block = lax.dot_general(
                q,
                window(group, slot, 0),
                (((1,), (1,)), ((), ())),
                preferred_element_type=jnp.float32,
            )
            for lane in range(0, rows, HEAD_DIM):
                part = block[:, lane : lane + HEAD_DIM].reshape(inside, tile, HEAD_DIM)
                part = jnp.where(masks[len(parts)], part, NEG).reshape(chunk, HEAD_DIM)
                parts.append(part)
                best = part if best is None else jnp.maximum(best, part)
        return parts, best

    def mix(index, c, i, parts, best, gathered):
        group = groups[index]
        top = jnp.max(best, axis=1, keepdims=True) * exponent
        mixed = None
        per_slot = rows // HEAD_DIM
        for slot in range(slots):
            probs = []
            for part in parts[per_slot * slot : per_slot * (slot + 1)]:
                weights = jnp.exp2(part * exponent - top)
                probs.append(weights.astype(jnp.bfloat16))
            values = jnp.concatenate([window(group, slot, 1), ones], axis=1)
            product = jnp.dot(
                jnp.concatenate(probs, axis=1), values, preferred_element_type=jnp.float32
            )
            mixed = product if mixed is None else mixed + product
        row_sum = mixed[:, HEAD_DIM:]
        result = (mixed[:, :HEAD_DIM] / row_sum).astype(jnp.bfloat16)
        norm = top * (1.0 / LOG2E) + jnp.log(row_sum)
        for h in range(inside):
            head = c * inside + h
            part = slice(h * tile, (h + 1) * tile)
            column_of = (index * per_group + head) * HEAD_DIM
            if unrolled:
                out_refs[i][:, column_of : column_of + HEAD_DIM] = result[part]
            else:
                staged[i, :, column_of : column_of + HEAD_DIM] = result[part]
            gathered = jnp.where(column == group * per_group + head, norm[part], gathered)
        return gathered

    def step(i, carry):
        t = lax.rem(z + tiles_of.start + i * tiles_of.step, tiles)
        here = pl.ds(pl.multiple_of(t * tile, tile), tile)
        gathered = norms[here, :]
        masks = masks_of(t)
        jobs = [(index, c) for index in range(len(groups)) for c in range(stacked // chunk)]
        ready = scores_of(groups[0], t, 0, masks)
        for job, (index, c) in enumerate(jobs):
            following = None
            if job + 1 < len(jobs):
                next_index, next_c = jobs[job + 1]
                following = scores_of(groups[next_index], t, next_c, masks)
            gathered = mix(index, c, i, *ready, gathered)
            ready = following
        norms[here, :] = gathered
        return carry

    if unrolled:
        for i in range(len(tiles_of)):
            step(i, 0)
    else:
        lax.fori_loop(0, len(tiles_of), step, 0)
        for position, out_ref in enumerate(out_refs):
            out_ref[...] = staged[position]
    if last:
        plan_copy.wait()
        shards = plan_ref.shape[0]
        block = rows // shards
        for s in range(shards):
            picked = pl.multiple_of(plan_ref[shard, s] * block, block)
            lse_ref[s * block : (s + 1) * block, :] = norms[pl.ds(picked, block), :]
    else:
        lse_ref[...] = norms[...]


def placed(planes, width, groups, places, pieces, out_ref, sems):
    z = lax.axis_index("kv")
    copies = []
    for index, (s, group) in enumerate(places):
        origin = lax.rem(z - s + planes, planes)
        column = pl.multiple_of((origin * groups + group) * width, width)
        target = out_ref.at[:, pl.ds(column, pieces[index].shape[1])]
        copies.append(pltpu.make_async_copy(pieces[index], target, sems.at[index]))
    return copies


def begin_kernel(planes, width, groups, places, *refs):
    pieces, out_ref, sems = refs[:-2], *refs[-2:]
    copies = placed(planes, width, groups, places, pieces, out_ref, sems)
    for c in copies:
        c.start()
    for c in copies:
        c.wait()


def assemble_kernel(planes, width, groups, places, served_ref, *refs):
    pieces, out_ref, lse_hbm, lse_ref, sems = refs[:-5], *refs[-4:]
    copies = placed(planes, width, groups, places, pieces, out_ref, sems)
    for c in copies:
        c.start()
    lse_ref[...] = served_ref[...].T[: lse_ref.shape[0]]
    lse_copy = pltpu.make_async_copy(lse_ref, lse_hbm, sems.at[len(pieces)])
    lse_copy.start()
    for c in copies:
        c.wait()
    lse_copy.wait()


def body(queries, key_states, value_states, doc_lengths, block_plan):
    shards = lax.axis_size("tok")
    planes = lax.axis_size("kv")
    rows = queries.shape[0]
    groups = key_states.shape[1] // HEAD_DIM
    heads = queries.shape[1] // HEAD_DIM
    per_group = heads // groups
    tile = rows // planes
    pieces = shards // 4
    half_freq = THETA ** (-np.arange(HALF, dtype=np.float64) * 2.0 / HEAD_DIM)
    freq = jnp.asarray(np.concatenate([half_freq, half_freq])[None, :], jnp.float32)

    pair = [(i, i ^ 1) for i in range(shards)]

    def forward(x, p):
        return lax.ppermute(x, "tok", [(i, i + 2 * p) for i in range(shards - 2 * p)])

    far_keys = [forward(key_states, p) for p in range(1, pieces + 1)]
    far_values = [forward(value_states, p) for p in range(1, pieces + 1)]
    relayed = []
    after = queries
    if shards == 8:
        far_keys[0] = lax.ppermute(key_states, "tok", [(0, 2), (1, 3), (4, 6), (5, 7)])
        relayed = [lax.ppermute(far_keys[1], "tok", [(6, 4), (7, 5)])]
        after, _ = lax.optimization_barrier((queries, far_keys[1]))
    pack_shape = jax.ShapeDtypeStruct((rows, 2 * groups * HEAD_DIM), jnp.bfloat16)
    with jax.named_scope("rotate"):
        result = pl.pallas_call(
            partial(queries_kernel, pieces),
            out_shape=[
                pack_shape,
                jax.ShapeDtypeStruct((rows, HEAD_DIM), jnp.int32),
                jax.ShapeDtypeStruct((2 * pieces, rows, HEAD_DIM), jnp.float32),
            ]
            + [jax.ShapeDtypeStruct((planes, per_group * tile, HEAD_DIM), jnp.bfloat16)] * groups,
            in_specs=[hbm()] * 5,
            out_specs=[vmem()] * (3 + groups),
            scratch_shapes=[
                pltpu.SMEM(doc_lengths.shape, jnp.int32),
                pltpu.VMEM(freq.shape, jnp.float32),
                pltpu.VMEM(key_states.shape, jnp.bfloat16),
                pltpu.VMEM(value_states.shape, jnp.bfloat16),
                pltpu.VMEM(queries.shape, jnp.bfloat16),
                pltpu.SemaphoreType.DMA((5,)),
            ],
            compiler_params=params(),
            cost_estimate=cost(3.0),
        )(
            pltpu.with_memory_space_constraint(doc_lengths, pltpu.HBM),
            pltpu.with_memory_space_constraint(freq, pltpu.HBM),
            pltpu.with_memory_space_constraint(key_states, pltpu.HBM),
            pltpu.with_memory_space_constraint(value_states, pltpu.HBM),
            pltpu.with_memory_space_constraint(after, pltpu.HBM),
        )
    own, start, tables = result[:3]
    turned = result[3:]
    with jax.named_scope("pack"):
        mine, give = pl.pallas_call(
            partial(pack_kernel, pieces),
            out_shape=[
                jax.ShapeDtypeStruct((count, *pack_shape.shape), jnp.bfloat16)
                for count in (pieces + 1, pieces)
            ],
            in_specs=[vmem()] * (2 + 2 * pieces + len(relayed)),
            out_specs=[vmem()] * 2,
            compiler_params=params(),
            cost_estimate=cost(1.0),
        )(tables, own, *far_keys, *far_values, *relayed)
    theirs = lax.ppermute(give, "tok", pair)

    def attend(norm, used, tiles_of, last, microseconds):
        plan = [pltpu.with_memory_space_constraint(block_plan, pltpu.HBM)] if last else []
        operands = [start] if norm is None else [start, norm]
        operands += [mine, theirs] + [turned[group] for group in used]
        tasks = len(tiles_of)
        width = len(used) * per_group * HEAD_DIM
        with jax.named_scope("attend"):
            result = pl.pallas_call(
                partial(
                    attend_kernel, pieces, per_group, used, tiles_of, norm is not None, last
                ),
                out_shape=[jax.ShapeDtypeStruct((tile, width), jnp.bfloat16)]
                * tasks
                + [jax.ShapeDtypeStruct((rows, HEAD_DIM), jnp.float32)],
                in_specs=[hbm()] * len(plan) + [vmem()] * len(operands),
                out_specs=[vmem()] * (tasks + 1),
                scratch_shapes=[
                    pltpu.VMEM((tasks, tile, width), jnp.bfloat16),
                    pltpu.VMEM((rows, HEAD_DIM), jnp.float32),
                ]
                + [pltpu.SMEM(block_plan.shape, jnp.int32), pltpu.SemaphoreType.DMA((1,))]
                * len(plan),
                compiler_params=params(),
                cost_estimate=cost(microseconds),
            )(*plan, *operands)
        return result[:tasks], result[tasks]

    def send(piece, s):
        return lax.ppermute(piece, "kv", [(i, (i + s) % planes) for i in range(planes)])

    norm, pieces_of = None, {}
    both = list(range(groups))
    middle = planes // 2
    spans = [range(middle, middle + 1), range(1, planes, 2)]
    spans += [range(s, s + 1) for s in range(2, planes, 2) if s != middle]
    for span in spans:
        result, norm = attend(norm, both, span, False, 4.0 * len(span))
        for s, piece in zip(span, result):
            pieces_of[s, 0] = send(piece, s)
    (piece,), norm = attend(norm, both, range(1), True, 4.0)
    pieces_of[0, 0] = piece
    block_rows = rows // shards
    served = lax.all_to_all(
        norm.reshape(shards, block_rows, HEAD_DIM), "tok", split_axis=0, concat_axis=0, tiled=True
    ).reshape(rows, HEAD_DIM)
    width = per_group * HEAD_DIM
    out_shape = jax.ShapeDtypeStruct((tile, planes * heads * HEAD_DIM), jnp.bfloat16)
    soon = [place for place in sorted(pieces_of) if place[0] in (0, planes // 2)]
    late = [place for place in sorted(pieces_of) if place not in soon]
    with jax.named_scope("begin"):
        begun = pl.pallas_call(
            partial(begin_kernel, planes, width, groups, soon),
            out_shape=out_shape,
            in_specs=[hbm()] * len(soon),
            out_specs=hbm(),
            scratch_shapes=[pltpu.SemaphoreType.DMA((len(soon),))],
            compiler_params=params(),
        )(*[pieces_of[place] for place in soon])
    with jax.named_scope("assemble"):
        attention_out, served_lse = pl.pallas_call(
            partial(assemble_kernel, planes, width, groups, late),
            out_shape=[out_shape, jax.ShapeDtypeStruct((heads, rows), jnp.float32)],
            in_specs=[vmem()] + [hbm()] * (len(late) + 1),
            out_specs=[hbm(), hbm()],
            scratch_shapes=[
                pltpu.VMEM((heads, rows), jnp.float32),
                pltpu.SemaphoreType.DMA((len(late) + 1,)),
            ],
            input_output_aliases={len(late) + 1: 0},
            compiler_params=params(),
        )(served, *[pieces_of[place] for place in late], begun)
    return (attention_out, served_lse)


def solution(mesh):
    return jax.shard_map(
        body,
        mesh=mesh,
        in_specs=(P("tok", "kv"), P("tok", "kv"), P("tok", "kv"), P(), P()),
        out_specs=(P(("tok", "kv"), None), P("kv", "tok")),
        check_vma=False,
    )
```

```python
import math
from functools import partial

import jax
import jax.numpy as jnp
import numpy as np
from jax import lax
from jax.experimental import pallas as pl
from jax.experimental.pallas import tpu as pltpu
from jax.sharding import PartitionSpec as P

HEAD_DIM = 128
HALF = HEAD_DIM // 2
THETA = 500000.0
NEG = -1e30
LOG2E = math.log2(math.e)
SCALE = 1.0 / math.sqrt(HEAD_DIM)
VMEM_LIMIT = 48 * 1024 * 1024


def vmem():
    return pl.BlockSpec(memory_space=pltpu.VMEM)


def smem():
    return pl.BlockSpec(memory_space=pltpu.SMEM)


def hbm():
    return pl.BlockSpec(memory_space=pl.ANY)


def far_hbm():
    return pl.BlockSpec(memory_space=pltpu.HBM)


def params():
    return pltpu.CompilerParams(vmem_limit_bytes=VMEM_LIMIT)


def cost(microseconds):
    return pl.CostEstimate(flops=int(microseconds * 1.15e9), bytes_accessed=0, transcendentals=0)


def doc_starts(lengths_ref, token):
    begin = jnp.int32(0)
    start = jnp.zeros_like(token)
    for doc in range(lengths_ref.shape[0] - 1):
        begin = begin + lengths_ref[doc]
        start = jnp.where(token >= begin, begin, start)
    return start


def rotary_tables(lengths_ref, freq_ref, rows, first):
    token = first + lax.broadcasted_iota(jnp.int32, (rows, HEAD_DIM), 0)
    start = doc_starts(lengths_ref, token)
    position = token - start
    angle = position.astype(jnp.float32) * freq_ref[...]
    lane = lax.broadcasted_iota(jnp.int32, (rows, HEAD_DIM), 1)
    sine = jnp.sin(angle)
    return jnp.cos(angle), jnp.where(lane < HALF, -sine, sine), start


def turn(block, cosine, sine):
    x = block.astype(jnp.float32)
    return (x * cosine + pltpu.roll(x, HALF, 1) * sine).astype(jnp.bfloat16)


def pack(out_ref, key_ref, value_ref, cosine, sine):
    for group in range(key_ref.shape[1] // HEAD_DIM):
        cols = slice(group * HEAD_DIM, (group + 1) * HEAD_DIM)
        place = 2 * group * HEAD_DIM
        out_ref[:, place : place + HEAD_DIM] = turn(key_ref[:, cols], cosine, sine)
        out_ref[:, place + HEAD_DIM : place + 2 * HEAD_DIM] = value_ref[:, cols]


def queries_kernel(pieces, lengths_hbm, freq_hbm, key_hbm, value_hbm, query_hbm, *refs):
    pack_ref, start_ref, table_ref = refs[:3]
    turn_refs = refs[3:-6]
    lengths_ref, freq_ref, key_ref, value_ref, query_ref, sems = refs[-6:]
    copies = [
        pltpu.make_async_copy(key_hbm, key_ref, sems.at[0]),
        pltpu.make_async_copy(value_hbm, value_ref, sems.at[1]),
        pltpu.make_async_copy(query_hbm, query_ref, sems.at[2]),
        pltpu.make_async_copy(lengths_hbm, lengths_ref, sems.at[3]),
        pltpu.make_async_copy(freq_hbm, freq_ref, sems.at[4]),
    ]
    for c in copies[::-1]:
        c.start()
    for c in copies[3:]:
        c.wait()
    rows = query_ref.shape[0]
    shard = lax.axis_index("tok")
    cosine, sine, start = rotary_tables(lengths_ref, freq_ref, rows, shard * rows)
    start_ref[...] = start
    for c in copies[:2]:
        c.wait()
    pack(pack_ref, key_ref, value_ref, cosine, sine)
    for p in range(1, pieces + 1):
        far_cosine, far_sine, _ = rotary_tables(lengths_ref, freq_ref, rows, (shard - 2 * p) * rows)
        table_ref[2 * p - 2] = far_cosine
        table_ref[2 * p - 1] = far_sine
    copies[2].wait()
    tiles, stacked, _ = turn_refs[0].shape
    tile = rows // tiles
    per_group = stacked // tile
    for group, out_ref in enumerate(turn_refs):
        for head in range(per_group):
            cols = pl.ds((group * per_group + head) * HEAD_DIM, HEAD_DIM)
            turned = turn(query_ref[:, cols], cosine, sine)
            for t in range(tiles):
                out_ref[t, head * tile : (head + 1) * tile, :] = turned[t * tile : (t + 1) * tile]


def pack_kernel(pieces, table_ref, own_ref, *refs):
    mine_ref, give_ref = refs[-2:]
    relayed = refs[2 * pieces : -2]
    shard = lax.axis_index("tok")
    mine_ref[0] = own_ref[...]
    for p in range(pieces):
        keys = refs[p][...]
        if relayed and not p:
            keys = jnp.where(shard // 2 == 2, relayed[0][...], keys)
        pack(
            mine_ref.at[p + 1],
            keys,
            refs[pieces + p][...],
            table_ref[2 * p],
            table_ref[2 * p + 1],
        )
    odd = lax.rem(shard, 2)
    for p in range(pieces):
        give_ref[p] = mine_ref[p + odd]


def attend_kernel(pieces, per_group, groups, tiles_of, begun, last, *refs):
    norm_ref = None
    if last:
        plan_hbm, refs = refs[0], refs[1:]
        plan_ref, plan_sem = refs[-2:]
        refs = refs[:-2]
        plan_copy = pltpu.make_async_copy(plan_hbm, plan_ref, plan_sem.at[0])
        plan_copy.start()
    start_ref, refs = refs[0], refs[1:]
    if begun:
        norm_ref, refs = refs[0], refs[1:]
    slots = 2 * pieces + 1
    tasks = len(tiles_of)
    mine_ref, theirs_ref = refs[:2]
    refs = refs[2:]
    query_refs, refs = dict(zip(groups, refs)), refs[len(groups) :]
    out_refs, lse_ref = refs[:tasks], refs[tasks]
    staged, norms = refs[tasks + 1 :]
    shard, z = lax.axis_index("tok"), lax.axis_index("kv")
    tiles, stacked, _ = query_refs[groups[0]].shape
    tile = stacked // per_group
    rows = tile * tiles
    def window(group, slot, part):
        place = (2 * group + part) * HEAD_DIM
        cols = slice(place, place + HEAD_DIM)
        back = slots - 1 - slot
        if back % 2 == 0:
            return mine_ref[back // 2, :, cols]
        return theirs_ref[back // 2, :, cols]

    first = shard * rows
    window_first = (shard - (slots - 1)) * rows
    exponent = SCALE * LOG2E
    column = lax.broadcasted_iota(jnp.int32, (tile, HEAD_DIM), 1)
    line = lax.broadcasted_iota(jnp.int32, (tile, HEAD_DIM), 0)
    chunk = min(stacked, 256)
    inside = chunk // tile
    ones = jnp.ones((rows, HEAD_DIM), jnp.bfloat16)
    unrolled = slots <= 5
    norms[...] = norm_ref[...] if begun else jnp.zeros(norms.shape, jnp.float32)

    def masks_of(t):
        start = start_ref[pl.ds(pl.multiple_of(t * tile, tile), tile), :]
        masks = []
        for slot in range(slots):
            begins = start - (window_first + slot * rows)
            for lane in range(0, rows, HEAD_DIM):
                allowed = column + lane >= begins
                if slot == slots - 1:
                    allowed = allowed & (column + lane <= line + t * tile)
                masks.append(allowed[None])
        return masks

    def scores_of(group, t, c, masks):
        q = query_refs[group][t, c * chunk : (c + 1) * chunk, :]
        parts, best = [], None
        for slot in range(slots):
            block = lax.dot_general(
                q,
                window(group, slot, 0),
                (((1,), (1,)), ((), ())),
                preferred_element_type=jnp.float32,
            )
            for lane in range(0, rows, HEAD_DIM):
                part = block[:, lane : lane + HEAD_DIM].reshape(inside, tile, HEAD_DIM)
                part = jnp.where(masks[len(parts)], part, NEG).reshape(chunk, HEAD_DIM)
                parts.append(part)
                best = part if best is None else jnp.maximum(best, part)
        return parts, best

    def mix(index, c, i, parts, best, gathered):
        group = groups[index]
        top = jnp.max(best, axis=1, keepdims=True) * exponent
        mixed = None
        per_slot = rows // HEAD_DIM
        for slot in range(slots):
            probs = []
            for part in parts[per_slot * slot : per_slot * (slot + 1)]:
                weights = jnp.exp2(part * exponent - top)
                probs.append(weights.astype(jnp.bfloat16))
            values = jnp.concatenate([window(group, slot, 1), ones], axis=1)
            product = jnp.dot(
                jnp.concatenate(probs, axis=1), values, preferred_element_type=jnp.float32
            )
            mixed = product if mixed is None else mixed + product
        row_sum = mixed[:, HEAD_DIM:]
        result = (mixed[:, :HEAD_DIM] * pl.reciprocal(row_sum)).astype(jnp.bfloat16)
        norm = top * (1.0 / LOG2E) + jnp.log(row_sum)
        for h in range(inside):
            head = c * inside + h
            part = slice(h * tile, (h + 1) * tile)
            column_of = (index * per_group + head) * HEAD_DIM
            if unrolled:
                out_refs[i][:, column_of : column_of + HEAD_DIM] = result[part]
            else:
                staged[i, :, column_of : column_of + HEAD_DIM] = result[part]
            gathered = jnp.where(column == group * per_group + head, norm[part], gathered)
        return gathered

    def step(i, carry):
        t = lax.rem(z + tiles_of.start + i * tiles_of.step, tiles)
        here = pl.ds(pl.multiple_of(t * tile, tile), tile)
        gathered = norms[here, :]
        masks = masks_of(t)
        jobs = [(index, c) for index in range(len(groups)) for c in range(stacked // chunk)]
        ready = scores_of(groups[0], t, 0, masks)
        for job, (index, c) in enumerate(jobs):
            following = None
            if job + 1 < len(jobs):
                next_index, next_c = jobs[job + 1]
                following = scores_of(groups[next_index], t, next_c, masks)
            gathered = mix(index, c, i, *ready, gathered)
            ready = following
        norms[here, :] = gathered
        return carry

    if unrolled:
        for i in range(len(tiles_of)):
            step(i, 0)
    else:
        lax.fori_loop(0, len(tiles_of), step, 0)
        for position, out_ref in enumerate(out_refs):
            out_ref[...] = staged[position]
    if last:
        plan_copy.wait()
        shards = plan_ref.shape[0]
        block = rows // shards
        for s in range(shards):
            picked = pl.multiple_of(plan_ref[shard, s] * block, block)
            lse_ref[s * block : (s + 1) * block, :] = norms[pl.ds(picked, block), :]
    else:
        lse_ref[...] = norms[...]


def placed(planes, width, groups, places, pieces, out_ref, sems):
    z = lax.axis_index("kv")
    copies = []
    for index, (s, group) in enumerate(places):
        origin = lax.rem(z - s + planes, planes)
        column = pl.multiple_of((origin * groups + group) * width, width)
        target = out_ref.at[:, pl.ds(column, pieces[index].shape[1])]
        copies.append(pltpu.make_async_copy(pieces[index], target, sems.at[index]))
    return copies


def begin_kernel(planes, width, groups, places, *refs):
    pieces, out_ref, sems = refs[:-2], *refs[-2:]
    copies = placed(planes, width, groups, places, pieces, out_ref, sems)
    for c in copies:
        c.start()
    for c in copies:
        c.wait()


def assemble_kernel(planes, width, groups, places, served_ref, *refs):
    pieces, out_ref, lse_hbm, lse_ref, sems = refs[:-5], *refs[-4:]
    copies = placed(planes, width, groups, places, pieces, out_ref, sems)
    for c in copies:
        c.start()
    lse_ref[...] = served_ref[...].T[: lse_ref.shape[0]]
    lse_copy = pltpu.make_async_copy(lse_ref, lse_hbm, sems.at[len(pieces)])
    lse_copy.start()
    for c in copies:
        c.wait()
    lse_copy.wait()


def body(queries, key_states, value_states, doc_lengths, block_plan):
    shards = lax.axis_size("tok")
    planes = lax.axis_size("kv")
    rows = queries.shape[0]
    groups = key_states.shape[1] // HEAD_DIM
    heads = queries.shape[1] // HEAD_DIM
    per_group = heads // groups
    tile = rows // planes
    pieces = shards // 4
    half_freq = THETA ** (-np.arange(HALF, dtype=np.float64) * 2.0 / HEAD_DIM)
    freq = jnp.asarray(np.concatenate([half_freq, half_freq])[None, :], jnp.float32)

    pair = [(i, i ^ 1) for i in range(shards)]

    def forward(x, p):
        return lax.ppermute(x, "tok", [(i, i + 2 * p) for i in range(shards - 2 * p)])

    far_keys = [forward(key_states, p) for p in range(1, pieces + 1)]
    far_values = [forward(value_states, p) for p in range(1, pieces + 1)]
    relayed = []
    after = queries
    if shards == 8:
        far_keys[0] = lax.ppermute(key_states, "tok", [(0, 2), (1, 3), (4, 6), (5, 7)])
        relayed = [lax.ppermute(far_keys[1], "tok", [(6, 4), (7, 5)])]
        after, _ = lax.optimization_barrier((queries, far_keys[1]))
    pack_shape = jax.ShapeDtypeStruct((rows, 2 * groups * HEAD_DIM), jnp.bfloat16)
    with jax.named_scope("rotate"):
        result = pl.pallas_call(
            partial(queries_kernel, pieces),
            out_shape=[
                pack_shape,
                jax.ShapeDtypeStruct((rows, HEAD_DIM), jnp.int32),
                jax.ShapeDtypeStruct((2 * pieces, rows, HEAD_DIM), jnp.float32),
            ]
            + [jax.ShapeDtypeStruct((planes, per_group * tile, HEAD_DIM), jnp.bfloat16)] * groups,
            in_specs=[hbm()] * 5,
            out_specs=[vmem()] * (3 + groups),
            scratch_shapes=[
                pltpu.SMEM(doc_lengths.shape, jnp.int32),
                pltpu.VMEM(freq.shape, jnp.float32),
                pltpu.VMEM(key_states.shape, jnp.bfloat16),
                pltpu.VMEM(value_states.shape, jnp.bfloat16),
                pltpu.VMEM(queries.shape, jnp.bfloat16),
                pltpu.SemaphoreType.DMA((5,)),
            ],
            compiler_params=params(),
            cost_estimate=cost(3.0),
        )(
            pltpu.with_memory_space_constraint(doc_lengths, pltpu.HBM),
            pltpu.with_memory_space_constraint(freq, pltpu.HBM),
            pltpu.with_memory_space_constraint(key_states, pltpu.HBM),
            pltpu.with_memory_space_constraint(value_states, pltpu.HBM),
            pltpu.with_memory_space_constraint(after, pltpu.HBM),
        )
    own, start, tables = result[:3]
    turned = result[3:]
    with jax.named_scope("pack"):
        mine, give = pl.pallas_call(
            partial(pack_kernel, pieces),
            out_shape=[
                jax.ShapeDtypeStruct((count, *pack_shape.shape), jnp.bfloat16)
                for count in (pieces + 1, pieces)
            ],
            in_specs=[vmem()] * (2 + 2 * pieces + len(relayed)),
            out_specs=[vmem()] * 2,
            compiler_params=params(),
            cost_estimate=cost(1.0),
        )(tables, own, *far_keys, *far_values, *relayed)
    theirs = lax.ppermute(give, "tok", pair)

    def attend(norm, used, tiles_of, last, microseconds):
        plan = [pltpu.with_memory_space_constraint(block_plan, pltpu.HBM)] if last else []
        operands = [start] if norm is None else [start, norm]
        operands += [mine, theirs] + [turned[group] for group in used]
        tasks = len(tiles_of)
        width = len(used) * per_group * HEAD_DIM
        with jax.named_scope("attend"):
            result = pl.pallas_call(
                partial(
                    attend_kernel, pieces, per_group, used, tiles_of, norm is not None, last
                ),
                out_shape=[jax.ShapeDtypeStruct((tile, width), jnp.bfloat16)]
                * tasks
                + [jax.ShapeDtypeStruct((rows, HEAD_DIM), jnp.float32)],
                in_specs=[hbm()] * len(plan) + [vmem()] * len(operands),
                out_specs=[vmem()] * (tasks + 1),
                scratch_shapes=[
                    pltpu.VMEM((tasks, tile, width), jnp.bfloat16),
                    pltpu.VMEM((rows, HEAD_DIM), jnp.float32),
                ]
                + [pltpu.SMEM(block_plan.shape, jnp.int32), pltpu.SemaphoreType.DMA((1,))]
                * len(plan),
                compiler_params=params(),
                cost_estimate=cost(microseconds),
            )(*plan, *operands)
        return result[:tasks], result[tasks]

    def send(piece, s):
        return lax.ppermute(piece, "kv", [(i, (i + s) % planes) for i in range(planes)])

    norm, pieces_of = None, {}
    both = list(range(groups))
    for span in (range(1, 2), range(2, planes)):
        result, norm = attend(norm, both, span, False, 4.0 * len(span))
        for s, piece in zip(span, result):
            pieces_of[s, 0] = send(piece, s)
    (piece,), norm = attend(norm, both, range(1), True, 4.0)
    pieces_of[0, 0] = piece
    block_rows = rows // shards
    served = lax.all_to_all(
        norm.reshape(shards, block_rows, HEAD_DIM), "tok", split_axis=0, concat_axis=0, tiled=True
    ).reshape(rows, HEAD_DIM)
    width = per_group * HEAD_DIM
    out_shape = jax.ShapeDtypeStruct((tile, planes * heads * HEAD_DIM), jnp.bfloat16)
    soon = [place for place in sorted(pieces_of) if place[0] < 2]
    late = [place for place in sorted(pieces_of) if place[0] >= 2]
    with jax.named_scope("begin"):
        begun = pl.pallas_call(
            partial(begin_kernel, planes, width, groups, soon),
            out_shape=out_shape,
            in_specs=[hbm()] * len(soon),
            out_specs=hbm(),
            scratch_shapes=[pltpu.SemaphoreType.DMA((len(soon),))],
            compiler_params=params(),
        )(*[pieces_of[place] for place in soon])
    with jax.named_scope("assemble"):
        attention_out, served_lse = pl.pallas_call(
            partial(assemble_kernel, planes, width, groups, late),
            out_shape=[out_shape, jax.ShapeDtypeStruct((heads, rows), jnp.float32)],
            in_specs=[vmem()] + [hbm()] * (len(late) + 1),
            out_specs=[hbm(), hbm()],
            scratch_shapes=[
                pltpu.VMEM((heads, rows), jnp.float32),
                pltpu.SemaphoreType.DMA((len(late) + 1,)),
            ],
            input_output_aliases={len(late) + 1: 0},
            compiler_params=params(),
        )(served, *[pieces_of[place] for place in late], begun)
    return (attention_out, served_lse)


def solution(mesh):
    return jax.shard_map(
        body,
        mesh=mesh,
        in_specs=(P("tok", "kv"), P("tok", "kv"), P("tok", "kv"), P(), P()),
        out_specs=(P(("tok", "kv"), None), P("kv", "tok")),
        check_vma=False,
    )
```
